32 devices in a mesh: dp: 16 (over z, y, x), mp: 2 (over core).
Axes of the slice: x: 2, y: 2, z: 4, core: 2. Of those that a mesh axis runs over, the one named last changes fastest.
Arguments:
- inputs: bfloat16 [16384, 1024], P(('dp', 'mp'))
- cotangent: bfloat16 [16384, 1024], P(('dp', 'mp')), may hold values from -6 to 6
- lengths: int32 [16, 4], P('dp'), may hold values from 64 to 512, as said below
- seq_order: int32 [16, 4], P('dp'), may hold values from 0 to 3, as said below
- w_qkv: bfloat16 [2, 3, 1024, 1024], P(None, None, 'dp', 'mp'), may hold values from -0.1875 to 0.1875
- w_out: bfloat16 [2, 1024, 1024], P(None, 'mp', 'dp'), may hold values from -1.5 to 1.5
- w_in: bfloat16 [2, 1024, 4096], P(None, 'dp', 'mp'), may hold values from -0.1875 to 0.1875
- w_back: bfloat16 [2, 4096, 1024], P(None, 'mp', 'dp'), may hold values from -0.09375 to 0.09375
- biases: bfloat16 [2, 6, 1024], P(None, None, 'dp'), may hold values from -2 to 2
- norm_gains: bfloat16 [2, 2, 1024], P(None, None, 'dp'), may hold values from 0.5 to 1.5
- hidden_bias: bfloat16 [2, 4, 1024], P(None, 'mp', 'dp'), may hold values from -2 to 2
Outputs:
- output: bfloat16 [16384, 1024], P(('dp', 'mp'))
- input_grad: float32 [16384, 1024], P(('dp', 'mp'))
- grad_qkv: float32 [2, 3, 1024, 1024], P(None, None, 'dp', 'mp')
- grad_out: float32 [2, 1024, 1024], P(None, 'mp', 'dp')
- grad_in: float32 [2, 1024, 4096], P(None, 'dp', 'mp')
- grad_back: float32 [2, 4096, 1024], P(None, 'mp', 'dp')
- grad_biases: float32 [2, 6, 1024], P(None, None, 'dp')
- grad_gains: float32 [2, 2, 1024], P(None, None, 'dp')
- grad_hidden_bias: float32 [2, 4, 1024], P(None, 'mp', 'dp')
- rms: float32 [2, 3], replicated
The draws below stay inside these ranges and needn't reach their ends.
Inputs may be any that keep to these rules, and one draw needn't show every extreme that they name: Each group's lengths sum to at most 1024; the sequence at place 2 of each group's balanced order has exactly 512 tokens. Each row of seq_order is a permutation of 0 to 3.
All inputs are finite; a program needn't handle non-finite values.
Results may differ from the reference program's by a relative error of at most 0.035.
Values may be sent and summed in bfloat16 or wider, within the bound.
A program may use at most 320 MiB of HBM per device.

```python
import jax
import jax.numpy as jnp
from jax import lax

D = 1024
HEADS = 16
HEAD_DIM = 64
FF = 4096
LAYERS = 2
LONGEST = 512
SEQS = 4
ROWS = 1024
GROUPS = 16
TOKENS = 16384


def permute_one(sub_key):
    return jax.random.permutation(sub_key, SEQS)


def shared_plan(key):
    key_perm, key_one, key_two, key_last = jax.random.split(key, 4)
    order_rows = jax.vmap(permute_one)(jax.random.split(key_perm, GROUPS)).astype(jnp.int32)
    first_len = jax.random.randint(key_one, (GROUPS,), LONGEST // 8, 3 * LONGEST // 8 + 1).astype(jnp.int32)
    second_len = jax.random.randint(key_two, (GROUPS,), LONGEST // 8, 3 * LONGEST // 8 + 1).astype(jnp.int32)
    last_len = jax.random.randint(key_last, (GROUPS,), LONGEST // 8, LONGEST // 4 + 1).astype(jnp.int32)
    longest = jnp.full((GROUPS,), LONGEST, jnp.int32)
    balanced = jnp.stack([first_len, second_len, longest, last_len], axis=1)
    labels = jnp.arange(SEQS, dtype=jnp.int32)
    picked = (order_rows[:, :, None] == labels[None, None, :]).astype(jnp.int32)
    given_len = jnp.sum(picked * balanced[:, :, None], axis=1).astype(jnp.int32)
    return (order_rows, given_len)


def draw_lengths(key, part):
    return shared_plan(key)[1]


def draw_seq_order(key, part):
    return shared_plan(key)[0]


def draw_inputs(key, part):
    key = jax.random.fold_in(key, 7)
    key_value = jax.random.fold_in(key, 0)
    entries = jax.random.normal(key_value, (TOKENS, D), jnp.float32)
    scales = 0.5 + 1.5 * jnp.arange(TOKENS, dtype=jnp.float32)[:, None] / TOKENS
    return (entries * scales).astype(jnp.bfloat16)


def levels(rng, extent, cuts, smallest, high):
    factor_of, own = 1.0, jax.random.fold_in(rng, 6)
    for dim, parts in cuts:
        heights = jnp.exp(jax.random.uniform(jax.random.fold_in(own, dim), (parts,), jnp.float32, smallest / len(cuts), high / len(cuts)))
        factor_of = factor_of * jnp.repeat(heights, extent[dim] // parts).reshape([-1 if axis == dim else 1 for axis in range(len(extent))])
    return factor_of


def gaussian(stream_key, extent, scale, bound, pieces=(), kind=jnp.bfloat16):
    values = scale * jax.random.normal(stream_key, extent, jnp.float32)
    if pieces:
        values = values * levels(stream_key, extent, pieces, -0.22, 0.18)
    return jnp.clip(values, -bound, bound).astype(kind)


def setup_inputs(seed: int = 0) -> dict:
    splits = jax.random.split(jax.random.key(seed), 12)
    return {
        "inputs": draw_inputs(jax.random.fold_in(splits[11], 71), 0),
        "cotangent": gaussian(splits[1], (TOKENS, D), 1.0, 6.0, ((0, 32),)),
        "lengths": draw_lengths(jax.random.fold_in(splits[11], 71), 0),
        "seq_order": draw_seq_order(jax.random.fold_in(splits[11], 71), 0),
        "w_qkv": gaussian(splits[4], (LAYERS, 3, D, D), D ** -0.5, 0.1875, ((2, 16), (3, 2))),
        "w_out": gaussian(splits[5], (LAYERS, D, D), (max(D // 64, 4)) ** -0.5, 1.5, ((1, 2), (2, 16))),
        "w_in": gaussian(splits[6], (LAYERS, D, FF), D ** -0.5, 0.1875, ((1, 16), (2, 2))),
        "w_back": gaussian(splits[7], (LAYERS, FF, D), FF ** -0.5, 0.09375, ((1, 2), (2, 16))),
        "biases": gaussian(splits[8], (LAYERS, 6, D), 0.3, 2.0, ((2, 16),)),
        "norm_gains": jnp.clip(1.0 + 0.1 * jax.random.normal(splits[9], (LAYERS, 2, D), jnp.float32), 0.5, 1.5).astype(jnp.bfloat16),
        "hidden_bias": gaussian(splits[10], (LAYERS, FF // D, D), 0.3, 2.0, ((1, 2), (2, 16))),
    }


@jax.custom_vjp
def low(v):
    return lax.optimization_barrier(v.astype(jnp.bfloat16)).astype(jnp.float32)

@jax.custom_vjp
def low_back(v):
    return v

def low_keep(v):
    return (low(v), None)

def low_pass(kept, grad):
    return (grad,)

def back_keep(v):
    return (v, None)

def back_low(kept, grad):
    return (low(grad),)
low.defvjp(low_keep, low_pass)
low_back.defvjp(back_keep, back_low)
layer_eps = 1e-12
half_root = 0.7071067811865476

def plan_rows(lengths, seq_order, total_rows):
    count = lengths.shape[0]
    labels = jnp.arange(count, dtype=jnp.int32)
    picked = (seq_order[:, None] == labels[None, :]).astype(jnp.int32)
    bal_len = lax.optimization_barrier(jnp.sum(picked * lengths[None, :], axis=1))
    bal_end = jnp.cumsum(bal_len).astype(jnp.int32)
    bal_start = bal_end - bal_len
    giv_end = jnp.cumsum(lengths).astype(jnp.int32)
    giv_start = giv_end - lengths
    row_ids = jnp.arange(total_rows, dtype=jnp.int32)
    bal_seg = lax.optimization_barrier(jnp.sum((bal_end[None, :] <= row_ids[:, None]).astype(jnp.int32), axis=1))
    giv_seg = lax.optimization_barrier(jnp.sum((giv_end[None, :] <= row_ids[:, None]).astype(jnp.int32), axis=1))
    shift_seq = lax.optimization_barrier(jnp.sum(picked * bal_start[:, None], axis=0)) - giv_start
    giv_hit = (giv_seg[:, None] == labels[None, :]).astype(jnp.int32)
    source = row_ids + lax.optimization_barrier(jnp.sum(giv_hit * shift_seq[None, :], axis=1))
    shift_pos = bal_start - lax.optimization_barrier(jnp.sum(picked * giv_start[None, :], axis=1))
    bal_hit = (bal_seg[:, None] == labels[None, :]).astype(jnp.int32)
    target = row_ids - lax.optimization_barrier(jnp.sum(bal_hit * shift_pos[None, :], axis=1))
    return (bal_seg, giv_seg, source.astype(jnp.int32), target.astype(jnp.int32))

def dense(left_mat, right_mat):
    return jnp.dot(left_mat, right_mat, precision=lax.Precision.HIGHEST)

def layer_norm(values, gain_vec, shift_vec):
    center = values - lax.optimization_barrier(jnp.mean(values, axis=-1, keepdims=True))
    variance = lax.optimization_barrier(jnp.mean(center * center, axis=-1, keepdims=True))
    return center * lax.rsqrt(variance + layer_eps) * gain_vec + shift_vec

def gelu_value(values):
    return 0.5 * values * (1.0 + lax.erf(values * half_root))

def layer_pass(stream, same_seq, w_proj, w_mix, w_up, w_down, bias_rows, gain_rows, hidden_vec):
    score_scale = HEAD_DIM ** (-0.5)
    stream_low = low(stream)
    queries = low(low_back(dense(stream_low, w_proj[0]) + bias_rows[0]))
    key_rows = low(low_back(dense(stream_low, w_proj[1])))
    values = low(low_back(dense(stream_low, w_proj[2]) + bias_rows[1]))
    query_heads = queries.reshape(ROWS, HEADS, HEAD_DIM)
    key_heads = key_rows.reshape(ROWS, HEADS, HEAD_DIM)
    value_heads = values.reshape(ROWS, HEADS, HEAD_DIM)
    scores = low_back(jnp.einsum('qhd,khd->hqk', query_heads, key_heads, precision=lax.Precision.HIGHEST) * score_scale)
    masked = jnp.where(same_seq[None], scores, -1e+30)
    peak = lax.optimization_barrier(jnp.max(masked, axis=-1, keepdims=True))
    shifted = jnp.exp(masked - peak)
    probs = shifted / lax.optimization_barrier(jnp.sum(shifted, axis=-1, keepdims=True))
    mixture = jnp.einsum('hqk,khd->qhd', low(probs), value_heads, precision=lax.Precision.HIGHEST).reshape(ROWS, D)
    branch = low_back(dense(low(low_back(mixture)), w_mix) + bias_rows[2])
    normed = layer_norm(stream + branch, gain_rows[0], bias_rows[3])
    hidden = low_back(dense(low(normed), w_up) + hidden_vec)
    active = low(gelu_value(hidden))
    second = low_back(dense(active, w_down) + bias_rows[4])
    result = layer_norm(normed + second, gain_rows[1], bias_rows[5])
    return (result, branch, second)

def group_pass(params, stream_rows, cot_rows, len_row, order_row):
    bal_seg, giv_seg, source, target = plan_rows(len_row, order_row, ROWS)
    same_seq = bal_seg[:, None] == bal_seg[None, :]
    valid_rows = (bal_seg < SEQS).astype(jnp.float32)[:, None]
    given_valid = (giv_seg < SEQS).astype(jnp.float32)[:, None]
    stream = stream_rows
    squares = []
    for layer_idx in range(LAYERS):
        w_proj, w_mix, w_up, w_down, bias_rows, gain_rows, hidden_rows = [member[layer_idx] for member in params]
        result, branch, second = layer_pass(stream, same_seq, w_proj, w_mix, w_up, w_down, bias_rows, gain_rows, hidden_rows.reshape(FF))
        squares.append(jnp.stack([jnp.sum(valid_rows * stream * stream), jnp.sum(valid_rows * branch * branch), jnp.sum(valid_rows * second * second)]))
        stream = result
    given_out = stream[source] * given_valid
    loss = jnp.sum(given_out * cot_rows)
    return (loss, (given_out, jnp.stack(squares), jnp.sum(valid_rows)))

def reference(inputs, cotangent, lengths, seq_order, w_qkv, w_out, w_in, w_back, biases, norm_gains, hidden_bias):
    params = (w_qkv.astype(jnp.float32), w_out.astype(jnp.float32), w_in.astype(jnp.float32), w_back.astype(jnp.float32), biases.astype(jnp.float32), norm_gains.astype(jnp.float32), hidden_bias.astype(jnp.float32))
    stream_in = inputs.astype(jnp.float32).reshape(GROUPS, ROWS, D)
    cot_all = cotangent.astype(jnp.float32).reshape(GROUPS, ROWS, D)
    checked = jax.checkpoint(group_pass)

    def whole(param_set, stream_set):

        def one_group(items):
            return checked(param_set, items[0], items[1], items[2], items[3])
        losses, extras = lax.map(one_group, (stream_set, cot_all, lengths, seq_order))
        return (jnp.sum(losses), extras)
    loss, pull_back, extras = jax.vjp(whole, params, stream_in, has_aux=True)
    param_grads, input_grad = pull_back(jnp.ones_like(loss))
    given_out, squares, counts = extras
    rms = jnp.sqrt(lax.optimization_barrier(jnp.sum(squares, axis=0)) / (jnp.sum(counts) * D))
    return (given_out.reshape(TOKENS, D).astype(jnp.bfloat16), input_grad.reshape(TOKENS, D), param_grads[0], param_grads[1], param_grads[2], param_grads[3], param_grads[4], param_grads[5], param_grads[6], rms)
```

```python
import functools

import jax
import jax.numpy as jnp
from jax import lax
from jax.experimental import pallas as pl
from jax.experimental.pallas import tpu as pltpu
from jax.sharding import PartitionSpec as P

HEADS = 16
HEAD_DIM = 64
LAYERS = 2
MESH = pl.DeviceIdType.MESH


layer_eps = 1e-12
half_root = 0.7071067811865476
density_scale = 0.3989422804014327


class Place:
    def __init__(self, n, stride):
        position = lax.axis_index("dp")
        me = lax.div(position, stride) if stride > 1 else position
        self.me = me
        self.n = n
        self.depth = n // 4
        self.z = lax.div(me, 4)
        self.q = lax.rem(me, 4)
        low_bit = lax.rem(me, 2)
        high_bit = lax.rem(lax.div(me, 2), 2)
        self.step_x = 1 - 2 * low_bit
        self.step_y = 2 - 4 * high_bit
        self.dev_x = {"dp": position + self.step_x * stride}
        self.dev_y = {"dp": position + self.step_y * stride}
        self.position = position
        self.stride = stride
        self.dev_up = self.dev_plane(self.z + 1)
        self.dev_down = self.dev_plane(self.z - 1)
        self.can_up = self.z < self.depth - 1
        self.can_down = self.z > 0

    def dev_plane(self, zz):
        return {"dp": self.position + (zz - self.z) * 4 * self.stride}

    def planes(self, act, begin, end):
        down = begin > end

        def both(d):
            pl.when(self.z + d < self.depth)(lambda: act(self.z + d))
            pl.when(self.z - d >= 0)(lambda: act(self.z - d))

        def step(i, _):
            both(begin - i if down else begin + i)
            return 0

        if begin == 0:
            act(self.z)
            begin = 1
        count = 0 if begin == 1 and end == 0 and not down else abs(begin - max(end, 1)) + 1
        if count == 1:
            both(begin)
        elif count:
            lax.fori_loop(0, count, step, 0)
        if end == 0 and down:
            act(self.z)

    def cuts(self):
        far = self.depth - 1
        ends = [far * i // 3 for i in range(4)]
        return [(a + 1, b) for a, b in zip(ends[:-1], ends[1:])]

    def shard(self, zz, dx=False, dy=False):
        idx = zz * 4 + self.q
        if dx:
            idx = idx + self.step_x
        if dy:
            idx = idx + self.step_y
        return idx


def greet(place, straight):
    barrier = pltpu.get_barrier_semaphore()

    def call(dev):
        pl.semaphore_signal(barrier, inc=1, device_id=dev, device_id_type=MESH)

    call({"mp": 1 - lax.axis_index("mp")})
    call(place.dev_x)
    call(place.dev_y)
    if straight:
        for step in range(1, place.depth):
            call(place.dev_plane(lax.rem(place.z + step, place.depth)))
        count = 2 + place.depth
    else:
        pl.when(place.can_up)(lambda: call(place.dev_up))
        pl.when(place.can_down)(lambda: call(place.dev_down))
        count = 3 + place.can_up.astype(jnp.int32) + place.can_down.astype(jnp.int32)
    pl.semaphore_wait(barrier, count)


def remote(src, dst, send_sem, recv_sem, dev):
    return pltpu.make_async_remote_copy(
        src_ref=src, dst_ref=dst, send_sem=send_sem, recv_sem=recv_sem, device_id=dev, device_id_type=MESH
    )


class ColumnFirst:
    SENDS, RECVS = 6, 5

    def __init__(self, place, src, dst, start, size, cut, send, recv):
        self.p = place
        self.src = src.at[:, pl.ds(start, size)]
        self.dst = dst
        self.cols = pl.ds(start, size)
        self.sides = (pl.ds(start, cut), pl.ds(start + cut, size - cut))
        self.send = send
        self.recv = recv

    def at(self, idx):
        return self.dst.at[idx, :, self.cols]

    def _spread(self, src, zz):
        dst = self.at(self.p.shard(zz))
        return (
            remote(src, dst, self.send.at[2, zz], self.recv.at[1, zz], self.p.dev_x),
            remote(src, dst, self.send.at[3, zz], self.recv.at[2, zz], self.p.dev_y),
        )

    def _hop(self, src, zz, up):
        dst = self.at(self.p.shard(zz))
        dev = self.p.dev_up if up else self.p.dev_down
        return remote(src, dst, self.send.at[0 if up else 1, zz], self.recv.at[0, zz], dev)

    def _corner(self, idx_x, idx_y, zz):
        top, bottom = self.dst.at[idx_x, :, self.sides[0]], self.dst.at[idx_y, :, self.sides[1]]
        return (
            remote(top, top, self.send.at[5, zz], self.recv.at[3, zz], self.p.dev_y),
            remote(bottom, bottom, self.send.at[4, zz], self.recv.at[4, zz], self.p.dev_x),
        )

    def _corner_out(self, zz):
        return self._corner(self.p.shard(zz, dx=True), self.p.shard(zz, dy=True), zz)

    def _corner_in(self, zz):
        idx = self.p.shard(zz, dx=True, dy=True)
        return self._corner(idx, idx, zz)

    def first(self):
        z = self.p.z
        for copy in self._spread(self.src, z):
            copy.start()
        pl.when(self.p.can_up)(lambda: self._hop(self.src, z, True).start())
        pl.when(self.p.can_down)(lambda: self._hop(self.src, z, False).start())

    def pass_corner(self, zz):
        a, b = self._corner_out(zz)
        ix, iy = self.at(self.p.shard(zz, dx=True)), self.at(self.p.shard(zz, dy=True))
        remote(ix, ix, self.send.at[2, zz], self.recv.at[1, zz], self.p.dev_x).wait_recv()
        a.start()
        remote(iy, iy, self.send.at[3, zz], self.recv.at[2, zz], self.p.dev_y).wait_recv()
        b.start()

    def spread_plane(self, zz):
        src = self.at(self.p.shard(zz))
        self._hop(src, zz, True).wait_recv()
        pl.when((zz < self.p.z) & self.p.can_up)(lambda: self._hop(src, zz, True).start())
        pl.when((zz > self.p.z) & self.p.can_down)(lambda: self._hop(src, zz, False).start())
        for copy in self._spread(src, zz):
            copy.start()

    def ticks(self):
        cuts = [(0, 0)] + self.p.cuts()

        def step(now, before):
            self.p.planes(self.spread_plane, *now)
            self.p.planes(self.pass_corner, *before)

        steps = [functools.partial(step, now, before) for now, before in zip(cuts[1:], cuts[:-1])]
        return steps + [lambda: self.p.planes(self.pass_corner, *cuts[-1]), self.finish]

    def finish(self):
        z = self.p.z

        def drain(zz):
            for copy in self._corner_in(zz):
                copy.wait_recv()
            for copy in self._corner_out(zz):
                copy.wait_send()
            src = self.at(self.p.shard(zz))
            for copy in self._spread(src, zz):
                copy.wait_send()
            pl.when((zz <= z) & self.p.can_up)(lambda: self._hop(src, zz, True).wait_send())
            pl.when((zz >= z) & self.p.can_down)(lambda: self._hop(src, zz, False).wait_send())

        self.p.planes(drain, 0, self.p.depth - 1)


class SquareFirst:
    OWN, X, Y, CORNER = range(4)

    def __init__(self, place, src, dst, start, size, cut, send, recv, hop_send, hop_recv):
        self.p = place
        self.src = src.at[:, pl.ds(start, size)]
        self.dst = dst
        self.cols = pl.ds(start, size)
        self.sides = (pl.ds(start, cut), pl.ds(start + cut, size - cut))
        self.send = send
        self.recv = recv
        self.hop_send = hop_send
        self.hop_recv = hop_recv

    def _idx(self, who, zz):
        return self.p.shard(zz, dx=who in (1, 3), dy=who in (2, 3))

    def at(self, who, zz):
        return self.dst.at[self._idx(who, zz), :, self.cols]

    def _own(self):
        dst = self.at(0, self.p.z)
        return (
            remote(self.src, dst, self.send.at[0], self.recv.at[0], self.p.dev_x),
            remote(self.src, dst, self.send.at[1], self.recv.at[1], self.p.dev_y),
        )

    def _corner(self, idx_x, idx_y):
        top, bottom = self.dst.at[idx_x, :, self.sides[0]], self.dst.at[idx_y, :, self.sides[1]]
        return (
            remote(top, top, self.send.at[3], self.recv.at[2], self.p.dev_y),
            remote(bottom, bottom, self.send.at[2], self.recv.at[3], self.p.dev_x),
        )

    def _corner_out(self):
        return self._corner(self._idx(1, self.p.z), self._idx(2, self.p.z))

    def _corner_in(self):
        idx = self._idx(3, self.p.z)
        return self._corner(idx, idx)

    def _hop(self, src, who, zz, up):
        dev = self.p.dev_up if up else self.p.dev_down
        return remote(
            src, self.at(who, zz), self.hop_send.at[0 if up else 1, who, zz], self.hop_recv.at[who, zz], dev
        )

    def _leave(self, src, who):
        z = self.p.z
        pl.when(self.p.can_up)(lambda: self._hop(src, who, z, True).start())
        pl.when(self.p.can_down)(lambda: self._hop(src, who, z, False).start())

    def _take(self, who, far, near):
        def act(zz):
            src = self.at(who, zz)
            self._hop(src, who, zz, True).wait_recv()
            pl.when((zz < self.p.z) & self.p.can_up)(lambda: self._hop(src, who, zz, True).start())
            pl.when((zz > self.p.z) & self.p.can_down)(lambda: self._hop(src, who, zz, False).start())

        self.p.planes(act, far, near)

    def first(self):
        for copy in self._own():
            copy.start()
        self._leave(self.src, 0)

    def _cross(self):
        z = self.p.z
        a, b = self._corner_out()
        ix, iy = self.at(1, z), self.at(2, z)
        remote(ix, ix, self.send.at[0], self.recv.at[0], self.p.dev_x).wait_recv()
        a.start()
        self._leave(ix, 1)
        remote(iy, iy, self.send.at[1], self.recv.at[1], self.p.dev_y).wait_recv()
        b.start()
        self._leave(iy, 2)

    def _corner_done(self):
        for copy in self._corner_in():
            copy.wait_recv()
        self._leave(self.at(3, self.p.z), 3)

    def ticks(self):
        one, two, three = self.p.cuts()

        def first():
            self._cross()
            self._take(0, *one)

        def second():
            self._take(1, *one)
            self._take(2, *one)
            self._take(0, *two)
            self._corner_done()

        def third():
            self._take(1, *two)
            self._take(2, *two)
            self._take(0, *three)
            self._take(3, *one)

        def fourth():
            self._take(1, *three)
            self._take(2, *three)
            self._take(3, *two)

        def last():
            self._take(3, *three)
            self.finish()

        return [first, second, third, fourth, last]

    def finish(self):
        z = self.p.z
        for copy in self._own() + self._corner_out():
            copy.wait_send()

        def drain(zz):
            for who in range(4):
                src = self.at(who, zz)
                pl.when((zz <= z) & self.p.can_up)(lambda: self._hop(src, who, zz, True).wait_send())
                pl.when((zz >= z) & self.p.can_down)(lambda: self._hop(src, who, zz, False).wait_send())

        self.p.planes(drain, 0, self.p.depth - 1)


class Gather:
    def __init__(self, place, src, dst, turn, column_sems, square_sems, own_sem):
        tiles = src.shape[1] // 128
        square = max(1, tiles * 3 // 16)
        column = tiles - square
        cut = (column + turn) // 2
        self.src = src
        self.mine = dst.at[place.me]
        self.own_sem = own_sem
        self.jobs = [ColumnFirst(place, src, dst, 0, column * 128, max(1, cut) * 128, *column_sems)]
        if square > 1:
            square_cut = (square + 1 - turn) // 2
            self.jobs.append(
                SquareFirst(place, src, dst, column * 128, square * 128, square_cut * 128, *square_sems)
            )

    def _own(self):
        return pltpu.make_async_copy(self.src, self.mine, self.own_sem)

    def first(self):
        for job in self.jobs:
            job.first()
        self._own().start()

    def ticks(self):
        rows = list(zip(*[job.ticks() for job in self.jobs]))

        def step(row):
            for tick in row:
                tick()

        steps = [functools.partial(step, row) for row in rows]
        return steps[:-1] + [lambda: (steps[-1](), self._own().wait())]


class Scatter:
    def __init__(self, place, out, g, bufs, sems):
        self.p = place
        self.g = g
        self.out = out
        self.r1, self.r2, self.rz = bufs[:3]
        self.s1, self.v1, self.s2, self.v2, self.sz, self.vz = sems[:6]
        size = g.shape[2]
        self.main = self.r2.shape[3]
        self.main_cols = pl.ds(0, self.main)
        self.sides = self._halves(0, self.main)
        self.square = len(bufs) > 3
        if self.square:
            self.pz, self.p1, self.p2 = bufs[3:]
            self.tz, self.uz, self.t1, self.u1, self.t2, self.u2 = sems[6:]
            self.square_cols = pl.ds(self.main, size - self.main)
            self.square_sides = self._halves(self.main, size - self.main)

    def _halves(self, start, size):
        return pl.ds(start, size // 2), pl.ds(start + size // 2, size // 2)

    def _corner(self, zz):
        ic = self.p.shard(zz, dx=True, dy=True)
        top, bottom = self.sides
        return (
            remote(self.g.at[ic, :, top], self.r1.at[zz, 0], self.s1.at[zz, 0], self.v1.at[zz, 0], self.p.dev_y),
            remote(self.g.at[ic, :, bottom], self.r1.at[zz, 1], self.s1.at[zz, 1], self.v1.at[zz, 1], self.p.dev_x),
        )

    def _across(self, zz):
        to_x = self.g.at[self.p.shard(zz, dx=True), :, self.main_cols]
        to_y = self.g.at[self.p.shard(zz, dy=True), :, self.main_cols]
        return (
            remote(to_x, self.r2.at[zz, 0], self.s2.at[zz, 0], self.v2.at[zz, 0], self.p.dev_x),
            remote(to_y, self.r2.at[zz, 1], self.s2.at[zz, 1], self.v2.at[zz, 1], self.p.dev_y),
        )

    def _plane(self, zz):
        src, slot = self.g.at[self.p.shard(zz), :, self.main_cols], self.p.z
        return remote(src, self.rz.at[slot], self.sz.at[zz], self.vz.at[slot], self.p.dev_plane(zz))

    def _plane_in(self, zz):
        return remote(self.rz.at[zz], self.rz.at[zz], self.sz.at[zz], self.vz.at[zz], self.p.dev_plane(zz))

    def _square_plane(self, zz):
        src, slot = self.g.at[pl.ds(zz * 4, 4), :, self.square_cols], self.p.z
        return remote(src, self.pz.at[slot], self.tz.at[zz], self.uz.at[slot], self.p.dev_plane(zz))

    def _square_plane_in(self, zz):
        return remote(self.pz.at[zz], self.pz.at[zz], self.tz.at[zz], self.uz.at[zz], self.p.dev_plane(zz))

    def _square_corner(self):
        ic = self.p.shard(self.p.z, dx=True, dy=True)
        top, bottom = self.square_sides
        return (
            remote(self.g.at[ic, :, top], self.p1.at[0], self.t1.at[0], self.u1.at[0], self.p.dev_y),
            remote(self.g.at[ic, :, bottom], self.p1.at[1], self.t1.at[1], self.u1.at[1], self.p.dev_x),
        )

    def _square_across(self):
        to_x = self.g.at[self.p.shard(self.p.z, dx=True), :, self.square_cols]
        to_y = self.g.at[self.p.shard(self.p.z, dy=True), :, self.square_cols]
        return (
            remote(to_x, self.p2.at[0], self.t2.at[0], self.u2.at[0], self.p.dev_x),
            remote(to_y, self.p2.at[1], self.t2.at[1], self.u2.at[1], self.p.dev_y),
        )

    def _add(self, idx, cols, extra):
        at = (idx, slice(None), cols)
        total = self.g[at].astype(jnp.float32)
        for more in extra:
            total = total + more.astype(jnp.float32)
        self.g[at] = total.astype(self.g.dtype)

    def send_corner(self):
        def act(zz):
            for copy in self._corner(zz):
                copy.start()

        self.p.planes(act, self.p.depth - 1, 0)
        if self.square:
            self.p.planes(lambda zz: self._square_plane(zz).start(), self.p.depth - 1, 1)

    def send_across(self, far, near):
        def act(zz):
            a, b = self._corner(zz)
            to_x, to_y = self._across(zz)
            a.wait_recv()
            b.wait_recv()
            self._add(self.p.shard(zz, dx=True), self.sides[0], [self.r1[zz, 0]])
            self._add(self.p.shard(zz, dy=True), self.sides[1], [self.r1[zz, 1]])
            to_x.start()
            to_y.start()

        self.p.planes(act, far, near)

    def square_cross(self):
        z, depth = self.p.z, self.p.depth
        at = (pl.ds(z * 4, 4), slice(None), self.square_cols)

        def take(step, total):
            zz = lax.rem(z + step, depth)
            self._square_plane_in(zz).wait_recv()
            return total + self.pz[zz].astype(F32)

        total = lax.fori_loop(1, depth, take, self.g[at].astype(F32))
        for step in range(1, depth):
            self._square_plane(lax.rem(z + step, depth)).wait_send()
        self.g[at] = total.astype(self.g.dtype)
        for copy in self._square_corner():
            copy.start()

    def square_across(self):
        for copy in self._square_corner():
            copy.wait_recv()
        for i in range(2):
            idx = self.p.shard(self.p.z, dx=i == 0, dy=i == 1)
            self._add(idx, self.square_sides[i], [self.p1[i]])
        for copy in self._square_across():
            copy.start()

    def send_planes(self, far, near):
        def act(zz):
            for copy in self._across(zz):
                copy.wait_recv()
            self._add(self.p.shard(zz), self.main_cols, [self.r2[zz, 0], self.r2[zz, 1]])
            self._plane(zz).start()

        self.p.planes(act, far, near)

    def finish(self):
        z, out = self.p.z, self.out
        for copy in self._across(z):
            copy.wait_recv()
        total = self.g[self.p.me, :, self.main_cols].astype(F32)
        out[:, self.main_cols] = total + self.r2[z, 0].astype(F32) + self.r2[z, 1].astype(F32)

        def take(zz):
            self._plane_in(zz).wait_recv()
            out[:, self.main_cols] += self.rz[zz].astype(F32)
            self._plane(zz).wait_send()

        def drain(zz):
            for copy in self._corner(zz) + self._across(zz):
                copy.wait_send()

        self.p.planes(take, self.p.depth - 1, 1)
        self.p.planes(drain, self.p.depth - 1, 0)
        if self.square:
            for copy in self._square_across():
                copy.wait_recv()
            total = self.g[self.p.me, :, self.square_cols].astype(F32)
            out[:, self.square_cols] = total + self.p2[0].astype(F32) + self.p2[1].astype(F32)
            for copy in self._square_corner() + self._square_across():
                copy.wait_send()

    def crossings(self):
        steps = [lambda: self.send_across(self.p.depth - 1, 1), lambda: self.send_across(0, 0)]
        if self.square:
            steps[1] = lambda: (self.send_across(0, 0), self.square_cross())
        return steps

    def lines(self):
        steps = [functools.partial(self.send_planes, far, near) for near, far in reversed(self.p.cuts())]
        if self.square:
            begin = steps[0]
            steps[0] = lambda: (self.square_across(), begin())
        return steps


def scatter_scratch(n, rows, cols, dtype):
    dma = pltpu.SemaphoreType.DMA
    depth = n // 4
    square = cols // 1024 * 128
    main = cols - square
    bufs = [
        pltpu.VMEM((depth, 2, rows, main // 2), dtype),
        pltpu.VMEM((depth, 2, rows, main), dtype),
        pltpu.VMEM((depth, rows, main), dtype),
    ]
    sems = [dma((depth, 2)), dma((depth, 2)), dma((depth, 2)), dma((depth, 2)), dma((depth,)), dma((depth,))]
    if square:
        bufs += [
            pltpu.VMEM((depth, 4, rows, square), dtype),
            pltpu.VMEM((2, rows, square // 2), dtype),
            pltpu.VMEM((2, rows, square), dtype),
        ]
        sems += [dma((depth,)), dma((depth,)), dma((2,)), dma((2,)), dma((2,)), dma((2,))]
    return [pltpu.VMEM((n, rows, cols), dtype), bufs, sems]


VMEM, SMEM, ANY = pltpu.VMEM, pltpu.SMEM, pl.ANY


class Beside:
    def __init__(self):
        self.left = []
        self.done = set()

    def add(self, name, ticks):
        self.left += [(None, tick) for tick in ticks[:-1]] + [(name, ticks[-1])]

    def _next(self):
        name, tick = self.left.pop(0)
        self.done.add(name)
        return tick

    def __call__(self, count=1):
        for _ in range(count):
            if self.left:
                self._next()()

    def in_loop(self, i, steps):
        for step in steps:
            if self.left:
                self._at(i == step, self._next())

    def _at(self, now, tick):
        @pl.when(now)
        def _():
            tick()

    def until(self, name):
        while name not in self.done:
            self()

    def rest(self):
        self(len(self.left))


AHEAD = 3


def gather_stream(beside, jobs, along):
    ticks = [job.ticks() for job in jobs]
    side = along.ticks()

    def both(k):
        ticks[0][k]()
        side[k]()

    steps = [[functools.partial(both, k) for k in range(5)]] + ticks[1:]
    for slot in range(3 * len(jobs) + 2):
        for u, job_steps in enumerate(steps):
            k = slot - 3 * u
            if 0 <= k < 5:
                beside.add(("gathered", u) if k == 4 else None, [job_steps[k]])
            if k == 2 and u + AHEAD < len(jobs):
                beside.add(None, [jobs[u + AHEAD].first])


BAL_END, GIV_END, SHIFT_SEQ, SHIFT_POS, TURN = 0, 4, 8, 12, 16
LOW = jnp.bfloat16
F32 = jnp.float32


def plan_numbers(lengths, seq_order):
    seqs = range(4)
    length = [lengths[j] for j in seqs]
    order = [seq_order[j] for j in seqs]

    def picked(values, place):
        return sum(jnp.where(order[place] == j, values[j], 0) for j in seqs)

    def ends(values):
        return [sum(values[: j + 1]) for j in seqs]

    bal_len = [picked(length, i) for i in seqs]
    bal_end, giv_end = ends(bal_len), ends(length)
    bal_start = [end - size for end, size in zip(bal_end, bal_len)]
    giv_start = [end - size for end, size in zip(giv_end, length)]
    shift_seq = [sum(jnp.where(order[i] == j, bal_start[i], 0) for i in seqs) - giv_start[j] for j in seqs]
    shift_pos = [bal_start[i] - picked(giv_start, i) for i in seqs]
    return bal_end + giv_end + shift_seq + shift_pos + [bal_start[2]]


def places(ends, position, plan):
    seg = jnp.zeros_like(position)
    for j in range(4):
        seg = seg + (position >= plan[ends + j]).astype(jnp.int32)
    return seg


def turned(row, plan, total):
    position = row + plan[TURN]
    return jnp.where(position >= total, position - total, position)


def turned_back(position, plan, total):
    row = position - plan[TURN]
    return jnp.where(row < 0, row + total, row)


def shifted(position, seg, first, plan, sign):
    for j in range(4):
        position = position + sign * jnp.where(seg == j, plan[first + j], 0)
    return position


def column(start, count):
    return start + lax.broadcasted_iota(jnp.int32, (count, 1), 0)


def pick_matrix(index, keep, total):
    lanes = lax.broadcasted_iota(jnp.int32, (index.shape[0], total), 1)
    index = jnp.where(keep, index, -1)
    return jnp.where(lanes == index, 1.0, 0.0).astype(LOW)


def dot(a, b):
    return jnp.dot(a, b, preferred_element_type=F32)


def dot_nt(a, b):
    return lax.dot_general(a, b, (((1,), (1,)), ((), ())), preferred_element_type=F32)


def dot_tn(a, b):
    return lax.dot_general(a, b, (((0,), (0,)), ((), ())), preferred_element_type=F32)


def loop(count, act):
    def step(i, _):
        act(i)
        return 0

    lax.fori_loop(0, count, step, 0)


def part(i, size):
    return pl.ds(pl.multiple_of(i * size, size), size)


def inside(base, i, size):
    return pl.ds(pl.multiple_of(base + i * size, size), size)


def to_partner(src, dst, sems, slot):
    return remote(src, dst, sems.at[0, slot], sems.at[1, slot], {"mp": 1 - lax.axis_index("mp")})


def mean_rows(values):
    return jnp.mean(values, axis=-1, keepdims=True)


CHUNK = 64
TILE = 512
ROW_GAIN, ROW_HIDDEN, ROW_SQUARE, ROW_COUNT, VEC_ROWS = 12, 16, 20, 26, 32


def head_lanes(h, size):
    lanes = lax.broadcasted_iota(jnp.int32, (1, 2 * size), 1)
    mine = lanes < size if h == 0 else lanes >= size
    return jnp.where(mine, 1.0, 0.0).astype(LOW)


def gelu_pair(u):
    rise = 0.5 * (1.0 + lax.erf(u * half_root))
    slope = rise + u * density_scale * jnp.exp(-0.5 * u * u)
    return (u * rise).astype(LOW), slope.astype(LOW)


def norm_chunk(z, gain, shift):
    center = z - mean_rows(z)
    inv = lax.rsqrt(mean_rows(center * center) + layer_eps)
    unit = center * inv
    return unit * gain + shift, unit, inv


def norm_back_chunk(grad, unit, inv, gain):
    scaled = grad * gain
    inner = scaled - mean_rows(scaled) - unit * mean_rows(scaled * unit)
    return inner * inv


def turn_over(src, dst):
    step = 256

    def tile(i):
        dst[:, part(i, step)] = src[part(i, step), :].T

    loop(src.shape[0] // step, tile)


def weight_rows(weight, j, count, cols):
    span = weight.shape[1]
    return weight[part(j, count // span), :, cols].reshape(count, -1)


def weight_cols(weight, cols):
    return weight[:, :, cols].reshape(weight.shape[0] * weight.shape[1], -1)


class Moves:
    def __init__(self, sems):
        self.sems = sems
        self.slots = {}
        self.open = {}

    def start(self, name, src, dst):
        slot = self.slots.setdefault(name, len(self.slots))
        self.open[name] = lambda: pltpu.make_async_copy(src, dst, self.sems.at[slot])
        self.open[name]().start()

    def wait(self, *names):
        for name in names:
            if name in self.open:
                self.open.pop(name)().wait()

    def wait_all(self):
        self.wait(*list(self.open))


def forward_kernel(n, stride, sizes, *refs):
    rows, total, width, cols, hidden = sizes
    units = 3 * LAYERS
    refs = list(refs)

    def take(count):
        taken = refs[:count]
        del refs[:count]
        return taken

    lengths, seq_order, x, cot, w_qkv, w_out, w_in, w_back, biases, gains, hidden_bias = take(11)
    x_out, qm_out, probs_out, y_out, act_out, slope_out, unit_out, inv_out = take(8)
    weights = take(units)
    vec, squares, dh = take(3)
    first_src, small, small_all = take(3)
    xs, qm, probs, wa, wi, wb, y_all, act, slope, unit, inv, stream, yf, held, sent, got, bias = take(17)
    pair_sems, move_sems, probs_sems, gather_sems = take(4)
    core = lax.axis_index("mp")
    base, other = core * rows, (1 - core) * rows
    own = part(core, rows)
    half = total // 2
    size = HEAD_DIM
    pair = 2 * size
    scale = HEAD_DIM ** (-0.5)
    slabs = cols // pair
    place = Place(n, stride)
    *gather_sems, own_sems = gather_sems
    plan = plan_numbers(lengths, seq_order)

    def pack_first(layer):
        for i in range(3):
            first_src[layer, :, pl.ds(i * cols, cols)] = w_qkv[layer, i]
        first_src[layer, :, pl.ds(3 * cols, cols)] = w_out[layer]

    pack_first(0)
    small[...] = jnp.zeros_like(small)
    span = w_in.shape[1]
    for layer in range(LAYERS):
        for row, values in ((6 * layer, biases), (ROW_GAIN + 2 * layer, gains), (ROW_HIDDEN + 2 * layer, hidden_bias)):
            for i in range(6 if values is biases else values.shape[1]):
                value = values[i, layer : layer + 1] if values is biases else values[layer, i : i + 1]
                small[row + i : row + i + 1, pl.ds(0, span)] = value.astype(F32)
    shards = []
    for layer in range(LAYERS):
        shards += [first_src.at[layer], w_in.at[layer], w_back.at[layer]]
    jobs = []
    for u, (src, dst) in enumerate(zip(shards + [small], weights + [small_all])):
        sems = [sem.at[u] for sem in gather_sems]
        jobs.append(Gather(place, src, dst, u % 2, sems[:2], sems[2:], own_sems.at[u]))
    greet(place, False)
    little = jobs.pop()
    little.first()
    for job in jobs[:AHEAD]:
        job.first()
    beside = Beside()
    gather_stream(beside, jobs, little)
    moves = Moves(move_sems)
    for layer in range(1, LAYERS):
        pack_first(layer)

    def fetch(u, where):
        beside.until(("gathered", u))
        moves.start(where, weights[u], {"wa": wa, "wi": wi, "wb": wb}[where])

    x_given, cot_given = pl.ds(0, width), pl.ds(width, width)
    copies = [
        to_partner(x, act.at[own, x_given], pair_sems, 4),
        to_partner(cot, act.at[own, cot_given], pair_sems, 5),
    ]
    for copy in copies:
        copy.start()
    act[own, x_given] = x[...]
    act[own, cot_given] = cot[...]
    squares[...] = jnp.zeros_like(squares)
    for copy in copies:
        copy.wait()
    beside()

    def turn(i):
        index = turned(column(i * TILE, TILE), plan, total)
        picks = pick_matrix(index, index >= 0, total)
        xs[0, part(i, TILE), :] = dot(picks, act[:, x_given]).astype(LOW)

    loop(total // TILE, turn)
    moves.start("x", xs.at[0], x_out.at[0])
    beside()
    position = turned(column(base, rows), plan, total)
    seg = places(BAL_END, position, plan)
    target = shifted(position, seg, SHIFT_POS, plan, -1)
    dh[...] = dot(pick_matrix(target, seg < 4, total), act[:, cot_given]).astype(LOW)
    stream[...] = xs[0, own, :].astype(F32)
    fetch(0, "wa")

    per = 128 // span
    from_lane = lax.broadcasted_iota(jnp.int32, (128, 128), 0)
    to_lane = lax.broadcasted_iota(jnp.int32, (128, 128), 1)

    def spread(j):
        lanes = 0.0
        for i in range(per):
            shift = jnp.where(to_lane == from_lane + i * span, 1.0, 0.0).astype(LOW)
            lanes = lanes + dot(small_all[j * per + i, :, pl.ds(0, 128)].astype(LOW), shift)
        vec[:, part(j, 128)] = lanes

    loop(width // 128, spread)

    back = turned(column(half, half), plan, total)
    seg_k = places(BAL_END, back, plan)
    across = turned(half + lax.broadcasted_iota(jnp.int32, (1, half), 1), plan, total)
    seg_q = places(BAL_END, across, plan)

    def valid(i):
        return places(BAL_END, turned(column(base + i * CHUNK, CHUNK), plan, total), plan) < 4

    for layer in range(LAYERS):
        x_all = xs.at[layer % 2]
        next_all = xs.at[(layer + 1) % 2]
        row = 6 * layer
        gain = ROW_GAIN + 2 * layer
        head_span = part(core, cols)
        bias[...] = jnp.zeros_like(bias)
        bias[0:1, pl.ds(0, cols)] = vec[row : row + 1, head_span]
        bias[0:1, pl.ds(2 * cols, cols)] = vec[row + 1 : row + 2, head_span]
        moves.wait_all()

        def project(t):
            m, j = lax.div(t, 3), lax.rem(t, 3)
            acc = dot(x_all[part(m, TILE), :], weight_cols(wa, part(j, cols)))
            qm[part(m, TILE), part(j, cols)] = (acc + bias[0:1, part(j, cols)]).astype(LOW)
            beside.in_loop(t, [3])

        loop(3 * (total // TILE), project)
        beside()

        def probs_move(s):
            slot = s % 2 if isinstance(s, int) else lax.rem(s, 2)
            return pltpu.make_async_copy(probs.at[slot], probs_out.at[layer, s], probs_sems.at[slot])

        def slab(s):
            slot = lax.rem(s, 2)

            @pl.when(s >= 2)
            def _():
                probs_move(s - 2).wait()

            for b in range(2):
                at = pl.ds(b * half, half)
                q = qm[at, part(s, pair)]
                k = qm[at, inside(cols, s, pair)]
                v = qm[at, inside(2 * cols, s, pair)]
                mixed = []
                for h in range(2):
                    lanes = head_lanes(h, size)
                    scores = dot_nt(k, q * (lanes * scale))
                    if b == 1:
                        scores = jnp.where(seg_k == seg_q, scores, -1e30)
                    peak = jnp.max(scores, axis=0, keepdims=True)
                    powers = jnp.exp(scores - peak)
                    share = (powers * (1.0 / jnp.sum(powers, axis=0, keepdims=True))).astype(LOW)
                    probs[slot, b, pl.ds(h * half, half), :] = share
                    mixed.append(dot_tn(v, share)[h * size : (h + 1) * size, :])
                qm[at, inside(3 * cols, s, pair)] = jnp.concatenate(mixed, axis=0).T.astype(LOW)
            probs_move(s).start()
            beside.in_loop(s, range(slabs))

        loop(slabs, slab)
        moves.start("qm", qm, qm_out.at[layer])
        for s in range(max(slabs - 2, 0), slabs):
            probs_move(s).wait()

        def out_of(left, left_cols, right, right_cols, slot):
            def product(at, j):
                return dot_nt(left[at, left_cols], weight_rows(right, j, TILE, right_cols))

            def far(j):
                sent[slot, :, part(j, TILE)] = product(part(1 - core, rows), j).astype(LOW)

            loop(width // TILE, far)
            copy = to_partner(sent.at[slot], got.at[slot], pair_sems, slot)
            copy.start()
            beside()

            def near(j):
                held[:, part(j, TILE)] = product(own, j)

            loop(width // TILE, near)
            copy.wait()

        mix_cols = pl.ds(3 * cols, cols)
        out_of(qm, mix_cols, wa, mix_cols, 0)

        def first_norm(i):
            at = part(i, CHUNK)
            h = stream[at, :]
            a = held[at, :] + got[0, at, :].astype(F32) + vec[row + 2 : row + 3, :]
            ok = jnp.where(valid(i), 1.0, 0.0)
            squares[3 * layer : 3 * layer + 1, :] += jnp.sum(ok * h * h, axis=0, keepdims=True)
            squares[3 * layer + 1 : 3 * layer + 2, :] += jnp.sum(ok * a * a, axis=0, keepdims=True)
            y, z, r = norm_chunk(h + a, vec[gain : gain + 1, :], vec[row + 3 : row + 4, :])
            unit[0, at, :] = z
            inv[0, at, :] = jnp.broadcast_to(r, (CHUNK, 128))
            yf[at, :] = y
            y_all[inside(base, i, CHUNK), :] = y.astype(LOW)

        loop(rows // CHUNK, first_norm)
        y_copy = to_partner(y_all.at[own], y_all.at[own], pair_sems, 2)
        y_copy.start()
        fetch(3 * layer + 1, "wi")
        moves.wait("wi")

        def raise_rows(start, at_steps):
            def tile(t):
                at, col = pl.ds(pl.multiple_of(start, rows), rows), part(t, TILE)
                hidden_row = ROW_HIDDEN + 2 * layer + lax.div(t, width // TILE)
                shift = vec[pl.ds(hidden_row, 1), part(lax.rem(t, width // TILE), TILE)]
                value, grad = gelu_pair(dot(y_all[at, :], weight_cols(wi, col)) + shift)
                act[at, col] = value
                slope[at, col] = grad
                beside.in_loop(t, at_steps)

            loop(hidden // TILE, tile)

        raise_rows(base, [1, 3])
        y_copy.wait()
        moves.start("y", y_all, y_out.at[layer])
        raise_rows(other, [1, 3])
        moves.start("act", act, act_out.at[layer])
        moves.start("slope", slope, slope_out.at[layer])
        fetch(3 * layer + 2, "wb")
        moves.wait("wb")
        out_of(act, slice(None), wb, slice(None), 1)
        beside()

        def second_norm(i):
            at = part(i, CHUNK)
            f = held[at, :] + got[1, at, :].astype(F32) + vec[row + 4 : row + 5, :]
            ok = jnp.where(valid(i), 1.0, 0.0)
            squares[3 * layer + 2 : 3 * layer + 3, :] += jnp.sum(ok * f * f, axis=0, keepdims=True)
            h, z, r = norm_chunk(yf[at, :] + f, vec[gain + 1 : gain + 2, :], vec[row + 5 : row + 6, :])
            unit[1, at, :] = z
            inv[1, at, :] = jnp.broadcast_to(r, (CHUNK, 128))
            stream[at, :] = h
            next_all[inside(base, i, CHUNK), :] = h.astype(LOW)

        loop(rows // CHUNK, second_norm)
        moves.start("unit", unit, unit_out.at[layer])
        moves.start("inv", inv, inv_out.at[layer])
        if layer + 1 < LAYERS:
            pass_on = to_partner(next_all.at[own], next_all.at[own], pair_sems, 3)
            pass_on.start()
            fetch(3 * layer + 3, "wa")
            pass_on.wait()
            moves.start("x", next_all, x_out.at[layer + 1])
        else:
            pass_on = to_partner(next_all.at[own], x_out.at[LAYERS, own], pair_sems, 3)
            pass_on.start()
            moves.start("x", next_all.at[own], x_out.at[LAYERS, own])
            pass_on.wait()
    beside.rest()
    moves.wait_all()


def forward(lengths, seq_order, x, cot, weights, vectors, n, stride, part_count):
    rows, width = x.shape
    total = rows * part_count
    span, hidden = weights[2].shape[1:]
    cols = weights[0].shape[3]
    shape = jax.ShapeDtypeStruct
    units = 3 * LAYERS
    half = total // 2
    slabs = cols // (2 * HEAD_DIM)
    dma = pltpu.SemaphoreType.DMA
    depth = n // 4
    vmem, smem, far = [pl.BlockSpec(memory_space=where) for where in (VMEM, SMEM, ANY)]
    outs = [
        shape((LAYERS + 1, total, width), LOW),
        shape((LAYERS, total, 4 * cols), LOW),
        shape((LAYERS, slabs, 2, 2 * half, half), LOW),
        shape((LAYERS, total, width), LOW),
        shape((LAYERS, total, hidden), LOW),
        shape((LAYERS, total, hidden), LOW),
        shape((LAYERS, 2, rows, width), F32),
        shape((LAYERS, 2, rows, 128), F32),
    ]
    outs += [shape((n, span, hidden), LOW)] * units
    outs += [
        shape((VEC_ROWS, width), F32),
        shape((8, width), F32),
        shape((rows, width), LOW),
    ]
    results = pl.pallas_call(
        functools.partial(forward_kernel, n, stride, (rows, total, width, cols, hidden)),
        out_shape=outs,
        in_specs=[smem, smem, vmem, vmem, vmem, vmem, far, far, vmem, vmem, vmem],
        out_specs=[far] * (8 + units) + [vmem] * 3,
        scratch_shapes=[
            VMEM((LAYERS, span, hidden), LOW),
            VMEM((VEC_ROWS, 256), F32),
            VMEM((n, VEC_ROWS, 256), F32),
            VMEM((2, total, width), LOW),
            VMEM((total, 4 * cols), LOW),
            VMEM((2, 2, 2 * half, half), LOW),
            VMEM((n, span, hidden), LOW),
            VMEM((n, span, hidden), LOW),
            VMEM((n, span, hidden), LOW),
            VMEM((total, width), LOW),
            VMEM((total, hidden), LOW),
            VMEM((total, hidden), LOW),
            VMEM((2, rows, width), F32),
            VMEM((2, rows, 128), F32),
            VMEM((rows, width), F32),
            VMEM((rows, width), F32),
            VMEM((rows, width), F32),
            VMEM((2, rows, width), LOW),
            VMEM((2, rows, width), LOW),
            VMEM((8, 3 * cols), F32),
            dma((2, 6)),
            dma((12,)),
            dma((2,)),
            [
                dma((units + 1, ColumnFirst.SENDS, depth)),
                dma((units + 1, ColumnFirst.RECVS, depth)),
                dma((units + 1, 4)),
                dma((units + 1, 4)),
                dma((units + 1, 2, 4, depth)),
                dma((units + 1, 4, depth)),
                dma((units + 1,)),
            ],
        ],
        compiler_params=pltpu.CompilerParams(
            collective_id=0, has_side_effects=True, vmem_limit_bytes=62 << 20
        ),
        name="forward",
    )(lengths, seq_order, x, cot, *weights, *vectors)
    return results[:8], results[8 : 8 + units], results[8 + units :]


def backward_kernel(n, stride, slot_count, sizes, *refs):
    rows, total, width, cols, hidden = sizes
    units = 3 * LAYERS
    refs = list(refs)

    def take(count):
        taken = refs[:count]
        del refs[:count]
        return taken

    lengths, seq_order, vec, squares, dh_in = take(5)
    plan = plan_numbers(lengths, seq_order)
    x_far, qm_far, probs_far, y_far, act_far, slope_far, unit_far, inv_far = take(8)
    weights = take(units)
    output, input_grad, grad_qkv, grad_out, grad_in, grad_back = take(6)
    own_small, partner_small = take(2)
    w1, w2, h1, h2, n1, sides, flip, probs = take(8)
    unit_rows, inv, dz, dh, sent, got, grads, staged = take(8)
    pair_sems, move_sems, probs_sems, read_sem = take(4)
    slots = take(slot_count)
    (little_refs,) = take(1)
    core = lax.axis_index("mp")
    base, other = core * rows, (1 - core) * rows
    own = part(core, rows)
    half = total // 2
    size = HEAD_DIM
    pair = 2 * size
    scale = HEAD_DIM ** (-0.5)
    slabs = cols // pair
    span = width // n
    place = Place(n, stride)
    moves = Moves(move_sems)
    crossings, lines = Beside(), Beside()
    jobs = [Scatter(place, staged, *slots[u % slot_count]) for u in range(units)]
    little = Scatter(place, own_small, *little_refs)

    def load_norm(layer):
        moves.start("unit", unit_far.at[layer, 1], unit_rows)
        moves.start("inv", inv_far.at[layer], inv)

    def free(u):
        if u >= slot_count:
            end(u - slot_count)

    def cross(u):
        crossings.until(u)

    def line(u, stage):
        crossings.until(u)
        lines.until((u, stage))

    def end(u):
        crossings.until(u)
        lines.until(u)

    def summed(u):
        job = jobs[u]
        job.send_corner()

        layer = last - u // 3
        if u % 3 == 2:
            targets = [(job.out.at[:, pl.ds(i * cols, cols)], grad_qkv.at[layer, i]) for i in range(3)]
            targets.append((job.out.at[:, pl.ds(3 * cols, cols)], grad_out.at[layer]))
        else:
            targets = [(job.out, (grad_back, grad_in)[u % 3].at[layer])]
        names = ["staged%d" % i for i in range(4)]

        def leave():
            moves.wait(*names)
            job.finish()
            for name, target in zip(names, targets):
                moves.start(name, *target)

        crossings.add(u, job.crossings())
        for stage, tick in enumerate(job.lines()):
            lines.add((u, stage), [tick])
        lines.add(u, [leave])

    last = LAYERS - 1
    moves.start("dh", dh_in, sent)
    load_norm(last)
    moves.start("w2", weights[3 * last + 2], w2)
    moves.start("h2", slope_far.at[last], h2)
    moves.start("h1", act_far.at[last], h1)
    moves.start("w1", weights[3 * last + 1], w1)
    moves.start("n1", y_far.at[last], n1)
    greet(place, True)
    grads[...] = jnp.zeros_like(grads)
    moves.wait("dh")

    def widen(i):
        dh[part(i, CHUNK), :] = sent[part(i, CHUNK), :].astype(F32)

    loop(rows // CHUNK, widen)

    def add_sum(row, values, lanes=slice(None)):
        grads[row : row + 1, lanes] += jnp.sum(values, axis=0, keepdims=True)

    for layer in reversed(range(LAYERS)):
        row = 6 * layer
        gain = ROW_GAIN + 2 * layer
        unit = 3 * (last - layer)
        moves.wait("unit", "inv")

        def second_norm(i):
            at = part(i, CHUNK)
            grad, z = dh[at, :], unit_rows[at, :]
            add_sum(gain + 1, grad * z)
            add_sum(row + 5, grad)
            out = norm_back_chunk(grad, z, inv[1, at, 0:1], vec[gain + 1 : gain + 2, :])
            dz[at, :] = out
            df = out.astype(LOW)
            add_sum(row + 4, df.astype(F32))
            sides[inside(base, i, CHUNK), :] = df

        loop(rows // CHUNK, second_norm)
        moves.start("unit", unit_far.at[layer, 0], unit_rows)
        if unit:
            pl.semaphore_wait(read_sem, 1)
        df_copy = to_partner(sides.at[own], sides.at[own], pair_sems, 0)
        df_copy.start()
        moves.wait("w2", "h2")

        def hidden_rows(start):
            def tile(t):
                at, col = pl.ds(pl.multiple_of(start, rows), rows), part(t, TILE)
                grad = (dot(sides[at, :], weight_cols(w2, col)) * h2[at, col].astype(F32)).astype(LOW)
                h2[at, col] = grad
                hidden_row = ROW_HIDDEN + 2 * layer + lax.div(t, width // TILE)
                grads[pl.ds(hidden_row, 1), part(lax.rem(t, width // TILE), TILE)] += jnp.sum(
                    grad.astype(F32), axis=0, keepdims=True
                )

            loop(hidden // TILE, tile)

        hidden_rows(base)
        df_copy.wait()
        turn_over(sides, flip)
        shards = TILE // span

        def outer(g, right, right_cols, g_cols, count, step):
            def tile(t):
                m, j = lax.div(t, count), lax.rem(t, count)
                value = dot(flip[part(m, TILE), :], right[:, inside(right_cols, j, step)])
                g[part(m, shards), :, inside(g_cols, j, step)] = value.astype(LOW).reshape(shards, span, step)

            loop((width // TILE) * count, tile)

        moves.wait("h1")
        free(unit)
        outer(jobs[unit].g, h1, 0, 0, hidden // TILE, TILE)
        summed(unit)
        if unit:
            line(unit - 2, 0)
        moves.start("h1", qm_far.at[layer], h1)
        hidden_rows(other)
        moves.start("w2", weights[3 * layer], w2)
        moves.wait("w1")

        def product(at, left, left_cols, right, right_cols, j):
            return dot_nt(left[at, left_cols], weight_rows(right, j, TILE, right_cols))

        every = slice(None)

        def far(j):
            sent[:, part(j, TILE)] = product(part(1 - core, rows), h2, every, w1, every, j).astype(LOW)

        loop(width // TILE, far)
        dy_copy = to_partner(sent, got, pair_sems, 1)
        dy_copy.start()

        def near(j):
            dh[:, part(j, TILE)] = product(own, h2, every, w1, every, j)

        loop(width // TILE, near)
        if unit:
            line(unit - 2, 1)
        moves.wait("unit")
        dy_copy.wait()

        def first_norm(i):
            at = part(i, CHUNK)
            grad, z = dz[at, :] + dh[at, :] + got[at, :].astype(F32), unit_rows[at, :]
            add_sum(gain, grad * z)
            add_sum(row + 3, grad)
            out = norm_back_chunk(grad, z, inv[0, at, 0:1], vec[gain : gain + 1, :])
            dz[at, :] = out
            da = out.astype(LOW)
            add_sum(row + 2, da.astype(F32))
            sides[inside(base, i, CHUNK), :] = da

        loop(rows // CHUNK, first_norm)
        da_copy = to_partner(sides.at[own], sides.at[own], pair_sems, 2)
        da_copy.start()
        if layer:
            load_norm(layer - 1)
            moves.start("w1", weights[3 * layer - 2], w1)
        if unit:
            line(unit - 2, 2)
            cross(unit - 1)
        else:
            cross(unit)
        free(unit + 1)
        moves.wait("n1")
        turn_over(n1, flip)
        moves.start("n1", x_far.at[layer], n1)
        outer(jobs[unit + 1].g, h2, 0, 0, hidden // TILE, TILE)
        summed(unit + 1)
        da_copy.wait()
        moves.wait("w2", "h1")
        mix_cols = pl.ds(3 * cols, cols)

        def probs_move(s, b):
            return pltpu.make_async_copy(probs_far.at[layer, s, b], probs.at[b], probs_sems.at[b])

        for b in range(2):
            probs_move(0, b).start()

        def mix_grad(m):
            value = dot(sides[part(m, TILE), :], weight_cols(w2, mix_cols))
            h2[part(m, TILE), mix_cols] = value.astype(LOW)

        loop(total // TILE, mix_grad)

        def slab(s):
            for b in range(2):
                at = pl.ds(b * half, half)
                q = h1[at, part(s, pair)]
                k = h1[at, inside(cols, s, pair)]
                v = h1[at, inside(2 * cols, s, pair)]
                do = h2[at, inside(3 * cols, s, pair)]
                inner = (do.astype(F32) * h1[at, inside(3 * cols, s, pair)].astype(F32)).T
                probs_move(s, b).wait()
                dq, dk, dv = [], 0.0, 0.0
                for h in range(2):
                    lanes = head_lanes(h, size)
                    mine = do * lanes
                    share = probs[b, pl.ds(h * half, half), :]
                    rowsum = jnp.sum(inner[h * size : (h + 1) * size, :], axis=0, keepdims=True)
                    ds = (share.astype(F32) * (dot_nt(v, mine) - rowsum)).astype(LOW)
                    dk = dk + dot(ds, q * (lanes * scale))
                    dv = dv + dot(share, mine)
                    dq.append(dot_tn(k, ds)[h * size : (h + 1) * size, :])

                @pl.when(s + 1 < slabs)
                def _(b=b):
                    probs_move(s + 1, b).start()

                dq = (jnp.concatenate(dq, axis=0) * scale).T.astype(LOW)
                dk, dv = dk.astype(LOW), dv.astype(LOW)
                h2[at, part(s, pair)] = dq
                h2[at, inside(cols, s, pair)] = dk
                h2[at, inside(2 * cols, s, pair)] = dv
                lanes_here = inside(core * cols, s, pair)
                add_sum(row, dq.astype(F32), lanes_here)
                add_sum(row + 1, dv.astype(F32), lanes_here)
            if unit:
                crossings.in_loop(s, [0, 0])
            lines.in_loop(s, [1, 2, 3])

        loop(slabs, slab)
        qkv_cols = pl.ds(0, 3 * cols)

        def far_input(j):
            value = product(part(1 - core, rows), h2, qkv_cols, w2, qkv_cols, j)
            sent[:, part(j, TILE)] = value.astype(LOW)

        loop(width // TILE, far_input)
        dh_copy = to_partner(sent, got, pair_sems, 3)
        dh_copy.start()

        def near_input(j):
            at = part(j, TILE)
            dh[:, at] = dz[:, at] + product(own, h2, qkv_cols, w2, qkv_cols, j)

        loop(width // TILE, near_input)
        if layer:
            moves.start("w2", weights[3 * layer - 1], w2)
        cross(unit + 1)
        free(unit + 2)
        g = jobs[unit + 2].g
        turn_over(sides, flip)
        if layer:
            pl.semaphore_signal(
                read_sem, inc=1, device_id={"mp": 1 - core}, device_id_type=MESH
            )
        outer(g, h1, 3 * cols, 3 * cols, 1, cols)
        if layer:
            moves.start("h1", act_far.at[layer - 1], h1)
        moves.wait("n1")
        turn_over(n1, flip)
        moves.start("n1", y_far.at[layer - 1] if layer else x_far.at[LAYERS], n1)
        outer(g, h2, 0, 0, 3, cols)
        summed(unit + 2)
        if layer:
            moves.start("h2", slope_far.at[layer - 1], h2)
        dh_copy.wait()

        def add_got(i):
            dh[part(i, CHUNK), :] += got[part(i, CHUNK), :].astype(F32)

        loop(rows // CHUNK, add_got)

    totals = jnp.sum(squares[0 : 3 * LAYERS, :], axis=1, keepdims=True)
    grads[ROW_SQUARE : ROW_SQUARE + 3 * LAYERS, :] = jnp.broadcast_to(totals, (3 * LAYERS, width))
    count = jnp.full((1, width), plan[BAL_END + 3], jnp.int32).astype(F32)
    grads[ROW_COUNT : ROW_COUNT + 1, :] = count
    per = 128 // span
    little.g[...] = jnp.zeros_like(little.g)

    def cut(j):
        lanes = grads[:, part(j, 128)]
        for i in range(per):
            little.g[j * per + i, :, pl.ds(0, 128)] = lanes

    loop(width // 128, cut)
    little.send_corner()

    dh_copy = to_partner(dh, unit_rows, pair_sems, 0)
    dh_copy.start()
    line(units - 3, 2)
    step = rows // 4
    moves.wait("n1")

    def give(i):
        given = column(base + i * step, step)
        seg = places(GIV_END, given, plan)
        source = turned_back(shifted(given, seg, SHIFT_SEQ, plan, 1), plan, total)
        sent[part(i, step), :] = dot(pick_matrix(source, seg < 4, total), n1[...]).astype(LOW)

    loop(4, give)
    moves.start("output", sent, output)
    dh_copy.wait()
    low_cols = pl.ds(0, width)

    def split(i):
        for start, values in ((base, dh), (other, unit_rows)):
            value = values[part(i, CHUNK), :]
            top = value.astype(LOW)
            at = inside(start, i, CHUNK)
            sides[at, :] = top
            h1[at, low_cols] = (value - top.astype(F32)).astype(LOW)

    loop(rows // CHUNK, split)

    def turn_back(i):
        back = turned_back(column(base + i * step, step), plan, total)
        picks = pick_matrix(back, back >= 0, total)
        dz[part(i, step), :] = dot(picks, sides[...]) + dot(picks, h1[:, low_cols])

    loop(4, turn_back)
    moves.start("input_grad", dz, input_grad)
    little_ticks = little.crossings() + little.lines() + [little.finish]
    for tick in little_ticks[:2]:
        tick()
    end(units - 3)
    cross(units - 1)
    for tick in little_ticks[2:]:
        tick()
    swap = to_partner(own_small, partner_small, pair_sems, 1)
    swap.start()
    end(units - 1)
    swap.wait()
    moves.wait_all()


def backward(lengths, seq_order, vec, squares, dh, kept, weights, n, stride):
    rows, width = dh.shape
    total, hidden = kept[4].shape[1:]
    slot_count = 3 if n <= 16 else 2
    span = weights[0].shape[1]
    cols = kept[1].shape[2] // 4
    units = len(weights)
    half = total // 2
    shape = jax.ShapeDtypeStruct
    dma = pltpu.SemaphoreType.DMA
    vmem, smem, far = [pl.BlockSpec(memory_space=where) for where in (VMEM, SMEM, ANY)]
    outs = [shape((rows, width), LOW), shape((rows, width), F32)]
    outs += [
        shape((LAYERS, 3, span, cols), F32),
        shape((LAYERS, span, cols), F32),
        shape((LAYERS, span, hidden), F32),
        shape((LAYERS, span, hidden), F32),
    ]
    outs += [shape((VEC_ROWS, 256), F32)] * 2
    results = pl.pallas_call(
        functools.partial(backward_kernel, n, stride, slot_count, (rows, total, width, cols, hidden)),
        out_shape=outs,
        in_specs=[smem, smem, vmem, vmem] + [far] * (9 + units),
        out_specs=[far] * 6 + [vmem] * 2,
        scratch_shapes=[
            VMEM((n, span, hidden), LOW),
            VMEM((n, span, hidden), LOW),
            VMEM((total, hidden), LOW),
            VMEM((total, hidden), LOW),
            VMEM((total, width), LOW),
            VMEM((total, width), LOW),
            VMEM((width, total), LOW),
            VMEM((2, 2 * half, half), LOW),
            VMEM((rows, width), F32),
            VMEM((2, rows, 128), F32),
            VMEM((rows, width), F32),
            VMEM((rows, width), F32),
            VMEM((rows, width), LOW),
            VMEM((rows, width), LOW),
            VMEM((VEC_ROWS, width), F32),
            VMEM((span, hidden), F32),
            dma((2, 4)),
            dma((20,)),
            dma((2,)),
            pltpu.SemaphoreType.REGULAR,
        ]
        + [scatter_scratch(n, span, hidden, LOW)] * slot_count
        + [scatter_scratch(n, VEC_ROWS, 256, F32)],
        compiler_params=pltpu.CompilerParams(
            collective_id=1, has_side_effects=True, vmem_limit_bytes=63 << 20
        ),
        name="backward",
    )(lengths, seq_order, vec, squares, dh, *kept, *weights)
    return results[:2], results[2:6], results[6:]


def grouped(values, stride, own):
    total = values
    for step in range(1, stride):
        n = lax.axis_size("dp")
        pairs = [(i, i - i % stride + (i + step) % stride) for i in range(n)]
        total = total + lax.ppermute(values, "dp", pairs)
    return total


def body(
    inputs,
    cotangent,
    lengths,
    seq_order,
    w_qkv,
    w_out,
    w_in,
    w_back,
    biases,
    norm_gains,
    hidden_bias,
):
    devices = lax.axis_size("dp")
    part_count = lax.axis_size("mp")
    width = inputs.shape[1]
    span = biases.shape[2]
    cols = w_qkv.shape[3]
    stride = max(1, 16 // span)
    n = devices // stride
    place_here = lax.axis_index("dp")

    def shared(values, axis):
        if stride == 1:
            return values
        shape = list(values.shape)
        size = shape[axis]
        shape[axis] = size * stride
        start = lax.rem(place_here, stride) * size
        return grouped(lax.dynamic_update_slice_in_dim(jnp.zeros(shape, values.dtype), values, start, axis), stride, 0)

    turned_out, turned_back = jnp.swapaxes(w_out, 1, 2), jnp.swapaxes(w_back, 1, 2)
    weights = [shared(w_qkv, 2), shared(turned_out, 1), shared(w_in, 1), shared(turned_back, 1)]
    vectors = [shared(vector, 2) for vector in (jnp.swapaxes(biases, 0, 1), norm_gains, hidden_bias)]
    lengths, seq_order = lengths.reshape(-1), seq_order.reshape(-1)
    kept, gathered, (vec, squares, dh) = forward(
        lengths, seq_order, inputs, cotangent, weights, vectors, n, stride, part_count
    )
    (output, input_grad), sums, (own_small, partner_small) = backward(
        lengths, seq_order, vec, squares, dh, kept, gathered, n, stride
    )

    if stride > 1:
        start = lax.rem(place_here, stride) * span
        sums = [lax.dynamic_slice_in_dim(grouped(sum_, stride, 0), start, span, sum_.ndim - 2) for sum_ in sums]
        own_small, partner_small = grouped(own_small, stride, 0), grouped(partner_small, stride, 0)
    both = own_small + partner_small
    lane = lax.rem(place_here, 128 // span) * span

    def lanes(values):
        return lax.dynamic_slice_in_dim(values, lane, span, 1)

    grad_biases = lanes(both[:ROW_GAIN]).reshape(biases.shape)
    grad_gains = lanes(both[ROW_GAIN:ROW_HIDDEN]).reshape(norm_gains.shape)
    grad_hidden_bias = lanes(own_small[ROW_HIDDEN:ROW_SQUARE]).reshape(hidden_bias.shape)
    valid_count = both[ROW_COUNT, 0] / part_count
    rms = jnp.sqrt(both[ROW_SQUARE:ROW_COUNT, 0] / (valid_count * width)).reshape(LAYERS, 3)

    grad_qkv, grad_out, grad_in, grad_back = sums
    grad_out, grad_back = jnp.swapaxes(grad_out, 1, 2), jnp.swapaxes(grad_back, 1, 2)
    return (
        output,
        input_grad,
        grad_qkv,
        grad_out,
        grad_in,
        grad_back,
        grad_biases,
        grad_gains,
        grad_hidden_bias,
        rms,
    )


def solution(mesh):
    in_specs = (
        P(("dp", "mp"), None),
        P(("dp", "mp"), None),
        P("dp", None),
        P("dp", None),
        P(None, None, "dp", "mp"),
        P(None, "mp", "dp"),
        P(None, "dp", "mp"),
        P(None, "mp", "dp"),
        P(None, None, "dp"),
        P(None, None, "dp"),
        P(None, "mp", "dp"),
    )
    out_specs = (
        P(("dp", "mp"), None),
        P(("dp", "mp"), None),
        P(None, None, "dp", "mp"),
        P(None, "mp", "dp"),
        P(None, "dp", "mp"),
        P(None, "mp", "dp"),
        P(None, None, "dp"),
        P(None, None, "dp"),
        P(None, "mp", "dp"),
        P(),
    )
    return jax.shard_map(body, mesh=mesh, in_specs=in_specs, out_specs=out_specs, check_vma=False)
```

```python
import functools

import jax
import jax.numpy as jnp
from jax import lax
from jax.experimental import pallas as pl
from jax.experimental.pallas import tpu as pltpu
from jax.sharding import PartitionSpec as P

HEADS = 16
HEAD_DIM = 64
LAYERS = 2
MESH = pl.DeviceIdType.MESH


layer_eps = 1e-12
half_root = 0.7071067811865476
density_scale = 0.3989422804014327


class Place:
    def __init__(self, n, stride):
        position = lax.axis_index("dp")
        me = lax.div(position, stride) if stride > 1 else position
        self.me = me
        self.n = n
        self.depth = n // 4
        self.z = lax.div(me, 4)
        self.q = lax.rem(me, 4)
        low_bit = lax.rem(me, 2)
        high_bit = lax.rem(lax.div(me, 2), 2)
        self.step_x = 1 - 2 * low_bit
        self.step_y = 2 - 4 * high_bit
        self.dev_x = {"dp": position + self.step_x * stride}
        self.dev_y = {"dp": position + self.step_y * stride}
        self.position = position
        self.stride = stride
        self.dev_up = self.dev_plane(self.z + 1)
        self.dev_down = self.dev_plane(self.z - 1)
        self.can_up = self.z < self.depth - 1
        self.can_down = self.z > 0

    def dev_plane(self, zz):
        return {"dp": self.position + (zz - self.z) * 4 * self.stride}

    def planes(self, act, begin, end):
        down = begin > end

        def both(d):
            pl.when(self.z + d < self.depth)(lambda: act(self.z + d))
            pl.when(self.z - d >= 0)(lambda: act(self.z - d))

        def step(i, _):
            both(begin - i if down else begin + i)
            return 0

        if begin == 0:
            act(self.z)
            begin = 1
        count = 0 if begin == 1 and end == 0 and not down else abs(begin - max(end, 1)) + 1
        if count == 1:
            both(begin)
        elif count:
            lax.fori_loop(0, count, step, 0)
        if end == 0 and down:
            act(self.z)

    def cuts(self):
        far = self.depth - 1
        ends = [far * i // 3 for i in range(4)]
        return [(a + 1, b) for a, b in zip(ends[:-1], ends[1:])]

    def shard(self, zz, dx=False, dy=False):
        idx = zz * 4 + self.q
        if dx:
            idx = idx + self.step_x
        if dy:
            idx = idx + self.step_y
        return idx


def greet(place, straight):
    barrier = pltpu.get_barrier_semaphore()

    def call(dev):
        pl.semaphore_signal(barrier, inc=1, device_id=dev, device_id_type=MESH)

    call({"mp": 1 - lax.axis_index("mp")})
    call(place.dev_x)
    call(place.dev_y)
    if straight:
        for step in range(1, place.depth):
            call(place.dev_plane(lax.rem(place.z + step, place.depth)))
        count = 2 + place.depth
    else:
        pl.when(place.can_up)(lambda: call(place.dev_up))
        pl.when(place.can_down)(lambda: call(place.dev_down))
        count = 3 + place.can_up.astype(jnp.int32) + place.can_down.astype(jnp.int32)
    pl.semaphore_wait(barrier, count)


def remote(src, dst, send_sem, recv_sem, dev):
    return pltpu.make_async_remote_copy(
        src_ref=src, dst_ref=dst, send_sem=send_sem, recv_sem=recv_sem, device_id=dev, device_id_type=MESH
    )


class ColumnFirst:
    SENDS, RECVS = 6, 5

    def __init__(self, place, src, dst, start, size, cut, send, recv):
        self.p = place
        self.src = src.at[:, pl.ds(start, size)]
        self.dst = dst
        self.cols = pl.ds(start, size)
        self.sides = (pl.ds(start, cut), pl.ds(start + cut, size - cut))
        self.send = send
        self.recv = recv

    def at(self, idx):
        return self.dst.at[idx, :, self.cols]

    def _spread(self, src, zz):
        dst = self.at(self.p.shard(zz))
        return (
            remote(src, dst, self.send.at[2, zz], self.recv.at[1, zz], self.p.dev_x),
            remote(src, dst, self.send.at[3, zz], self.recv.at[2, zz], self.p.dev_y),
        )

    def _hop(self, src, zz, up):
        dst = self.at(self.p.shard(zz))
        dev = self.p.dev_up if up else self.p.dev_down
        return remote(src, dst, self.send.at[0 if up else 1, zz], self.recv.at[0, zz], dev)

    def _corner(self, idx_x, idx_y, zz):
        top, bottom = self.dst.at[idx_x, :, self.sides[0]], self.dst.at[idx_y, :, self.sides[1]]
        return (
            remote(top, top, self.send.at[5, zz], self.recv.at[3, zz], self.p.dev_y),
            remote(bottom, bottom, self.send.at[4, zz], self.recv.at[4, zz], self.p.dev_x),
        )

    def _corner_out(self, zz):
        return self._corner(self.p.shard(zz, dx=True), self.p.shard(zz, dy=True), zz)

    def _corner_in(self, zz):
        idx = self.p.shard(zz, dx=True, dy=True)
        return self._corner(idx, idx, zz)

    def first(self):
        z = self.p.z
        for copy in self._spread(self.src, z):
            copy.start()
        pl.when(self.p.can_up)(lambda: self._hop(self.src, z, True).start())
        pl.when(self.p.can_down)(lambda: self._hop(self.src, z, False).start())

    def pass_corner(self, zz):
        a, b = self._corner_out(zz)
        ix, iy = self.at(self.p.shard(zz, dx=True)), self.at(self.p.shard(zz, dy=True))
        remote(ix, ix, self.send.at[2, zz], self.recv.at[1, zz], self.p.dev_x).wait_recv()
        a.start()
        remote(iy, iy, self.send.at[3, zz], self.recv.at[2, zz], self.p.dev_y).wait_recv()
        b.start()

    def spread_plane(self, zz):
        src = self.at(self.p.shard(zz))
        self._hop(src, zz, True).wait_recv()
        pl.when((zz < self.p.z) & self.p.can_up)(lambda: self._hop(src, zz, True).start())
        pl.when((zz > self.p.z) & self.p.can_down)(lambda: self._hop(src, zz, False).start())
        for copy in self._spread(src, zz):
            copy.start()

    def ticks(self):
        cuts = [(0, 0)] + self.p.cuts()

        def step(now, before):
            self.p.planes(self.spread_plane, *now)
            self.p.planes(self.pass_corner, *before)

        steps = [functools.partial(step, now, before) for now, before in zip(cuts[1:], cuts[:-1])]
        return steps + [lambda: self.p.planes(self.pass_corner, *cuts[-1]), self.finish]

    def finish(self):
        def take(zz):
            for copy in self._corner_in(zz):
                copy.wait_recv()

        self.p.planes(take, 0, self.p.depth - 1)

    def drain(self):
        z = self.p.z

        def drain(zz):
            for copy in self._corner_out(zz):
                copy.wait_send()
            src = self.at(self.p.shard(zz))
            for copy in self._spread(src, zz):
                copy.wait_send()
            pl.when((zz <= z) & self.p.can_up)(lambda: self._hop(src, zz, True).wait_send())
            pl.when((zz >= z) & self.p.can_down)(lambda: self._hop(src, zz, False).wait_send())

        self.p.planes(drain, 0, self.p.depth - 1)


class SquareFirst:
    OWN, X, Y, CORNER = range(4)

    def __init__(self, place, src, dst, start, size, cut, send, recv, hop_send, hop_recv):
        self.p = place
        self.src = src.at[:, pl.ds(start, size)]
        self.dst = dst
        self.cols = pl.ds(start, size)
        self.sides = (pl.ds(start, cut), pl.ds(start + cut, size - cut))
        self.send = send
        self.recv = recv
        self.hop_send = hop_send
        self.hop_recv = hop_recv

    def _idx(self, who, zz):
        return self.p.shard(zz, dx=who in (1, 3), dy=who in (2, 3))

    def at(self, who, zz):
        return self.dst.at[self._idx(who, zz), :, self.cols]

    def _own(self):
        dst = self.at(0, self.p.z)
        return (
            remote(self.src, dst, self.send.at[0], self.recv.at[0], self.p.dev_x),
            remote(self.src, dst, self.send.at[1], self.recv.at[1], self.p.dev_y),
        )

    def _corner(self, idx_x, idx_y):
        top, bottom = self.dst.at[idx_x, :, self.sides[0]], self.dst.at[idx_y, :, self.sides[1]]
        return (
            remote(top, top, self.send.at[3], self.recv.at[2], self.p.dev_y),
            remote(bottom, bottom, self.send.at[2], self.recv.at[3], self.p.dev_x),
        )

    def _corner_out(self):
        return self._corner(self._idx(1, self.p.z), self._idx(2, self.p.z))

    def _corner_in(self):
        idx = self._idx(3, self.p.z)
        return self._corner(idx, idx)

    def _hop(self, src, who, zz, up):
        dev = self.p.dev_up if up else self.p.dev_down
        return remote(
            src, self.at(who, zz), self.hop_send.at[0 if up else 1, who, zz], self.hop_recv.at[who, zz], dev
        )

    def _leave(self, src, who):
        z = self.p.z
        pl.when(self.p.can_up)(lambda: self._hop(src, who, z, True).start())
        pl.when(self.p.can_down)(lambda: self._hop(src, who, z, False).start())

    def _take(self, who, far, near):
        def act(zz):
            src = self.at(who, zz)
            self._hop(src, who, zz, True).wait_recv()
            pl.when((zz < self.p.z) & self.p.can_up)(lambda: self._hop(src, who, zz, True).start())
            pl.when((zz > self.p.z) & self.p.can_down)(lambda: self._hop(src, who, zz, False).start())

        self.p.planes(act, far, near)

    def first(self):
        for copy in self._own():
            copy.start()
        self._leave(self.src, 0)

    def _cross(self):
        z = self.p.z
        a, b = self._corner_out()
        ix, iy = self.at(1, z), self.at(2, z)
        remote(ix, ix, self.send.at[0], self.recv.at[0], self.p.dev_x).wait_recv()
        a.start()
        self._leave(ix, 1)
        remote(iy, iy, self.send.at[1], self.recv.at[1], self.p.dev_y).wait_recv()
        b.start()
        self._leave(iy, 2)

    def _corner_done(self):
        for copy in self._corner_in():
            copy.wait_recv()
        self._leave(self.at(3, self.p.z), 3)

    def ticks(self):
        one, two, three = self.p.cuts()

        def first():
            self._cross()
            self._take(0, *one)

        def second():
            self._take(1, *one)
            self._take(2, *one)
            self._take(0, *two)
            self._corner_done()

        def third():
            self._take(1, *two)
            self._take(2, *two)
            self._take(0, *three)
            self._take(3, *one)

        def fourth():
            self._take(1, *three)
            self._take(2, *three)
            self._take(3, *two)

        return [first, second, third, fourth, lambda: self._take(3, *three)]

    def drain(self):
        z = self.p.z
        for copy in self._own() + self._corner_out():
            copy.wait_send()

        def drain(zz):
            for who in range(4):
                src = self.at(who, zz)
                pl.when((zz <= z) & self.p.can_up)(lambda: self._hop(src, who, zz, True).wait_send())
                pl.when((zz >= z) & self.p.can_down)(lambda: self._hop(src, who, zz, False).wait_send())

        self.p.planes(drain, 0, self.p.depth - 1)


class Gather:
    def __init__(self, place, src, dst, turn, column_sems, square_sems, own_sem):
        tiles = src.shape[1] // 128
        square = max(1, tiles * 3 // 16)
        column = tiles - square
        cut = (column + turn) // 2
        self.src = src
        self.mine = dst.at[place.me]
        self.own_sem = own_sem
        self.jobs = [ColumnFirst(place, src, dst, 0, column * 128, max(1, cut) * 128, *column_sems)]
        if square > 1:
            square_cut = (square + 1 - turn) // 2
            self.jobs.append(
                SquareFirst(place, src, dst, column * 128, square * 128, square_cut * 128, *square_sems)
            )

    def _own(self):
        return pltpu.make_async_copy(self.src, self.mine, self.own_sem)

    def first(self):
        for job in self.jobs:
            job.first()
        self._own().start()

    def ticks(self):
        rows = list(zip(*[job.ticks() for job in self.jobs]))

        def step(row):
            for tick in row:
                tick()

        steps = [functools.partial(step, row) for row in rows]
        return steps[:-1] + [lambda: (steps[-1](), self._own().wait())]

    def drain(self):
        for job in self.jobs:
            job.drain()


class Scatter:
    def __init__(self, place, out, g, bufs, sems):
        self.p = place
        self.g = g
        self.out = out
        self.r1, self.r2, self.rz = bufs[:3]
        self.s1, self.v1, self.s2, self.v2, self.sz, self.vz = sems[:6]
        size = g.shape[2]
        self.main = self.r2.shape[3]
        self.main_cols = pl.ds(0, self.main)
        self.sides = self._halves(0, self.main)
        self.square = len(bufs) > 3
        if self.square:
            self.pz, self.p1, self.p2 = bufs[3:]
            self.tz, self.uz, self.t1, self.u1, self.t2, self.u2 = sems[6:]
            self.square_cols = pl.ds(self.main, size - self.main)
            self.square_sides = self._halves(self.main, size - self.main)

    def _halves(self, start, size):
        return pl.ds(start, size // 2), pl.ds(start + size // 2, size // 2)

    def _corner(self, zz):
        ic = self.p.shard(zz, dx=True, dy=True)
        top, bottom = self.sides
        return (
            remote(self.g.at[ic, :, top], self.r1.at[zz, 0], self.s1.at[zz, 0], self.v1.at[zz, 0], self.p.dev_y),
            remote(self.g.at[ic, :, bottom], self.r1.at[zz, 1], self.s1.at[zz, 1], self.v1.at[zz, 1], self.p.dev_x),
        )

    def _across(self, zz):
        to_x = self.g.at[self.p.shard(zz, dx=True), :, self.main_cols]
        to_y = self.g.at[self.p.shard(zz, dy=True), :, self.main_cols]
        return (
            remote(to_x, self.r2.at[zz, 0], self.s2.at[zz, 0], self.v2.at[zz, 0], self.p.dev_x),
            remote(to_y, self.r2.at[zz, 1], self.s2.at[zz, 1], self.v2.at[zz, 1], self.p.dev_y),
        )

    def _plane(self, zz):
        src, slot = self.g.at[self.p.shard(zz), :, self.main_cols], self.p.z
        return remote(src, self.rz.at[slot], self.sz.at[zz], self.vz.at[slot], self.p.dev_plane(zz))

    def _plane_in(self, zz):
        return remote(self.rz.at[zz], self.rz.at[zz], self.sz.at[zz], self.vz.at[zz], self.p.dev_plane(zz))

    def _square_plane(self, zz):
        src, slot = self.g.at[pl.ds(zz * 4, 4), :, self.square_cols], self.p.z
        return remote(src, self.pz.at[slot], self.tz.at[zz], self.uz.at[slot], self.p.dev_plane(zz))

    def _square_plane_in(self, zz):
        return remote(self.pz.at[zz], self.pz.at[zz], self.tz.at[zz], self.uz.at[zz], self.p.dev_plane(zz))

    def _square_corner(self):
        ic = self.p.shard(self.p.z, dx=True, dy=True)
        top, bottom = self.square_sides
        return (
            remote(self.g.at[ic, :, top], self.p1.at[0], self.t1.at[0], self.u1.at[0], self.p.dev_y),
            remote(self.g.at[ic, :, bottom], self.p1.at[1], self.t1.at[1], self.u1.at[1], self.p.dev_x),
        )

    def _square_across(self):
        to_x = self.g.at[self.p.shard(self.p.z, dx=True), :, self.square_cols]
        to_y = self.g.at[self.p.shard(self.p.z, dy=True), :, self.square_cols]
        return (
            remote(to_x, self.p2.at[0], self.t2.at[0], self.u2.at[0], self.p.dev_x),
            remote(to_y, self.p2.at[1], self.t2.at[1], self.u2.at[1], self.p.dev_y),
        )

    def _add(self, idx, cols, extra):
        at = (idx, slice(None), cols)
        total = self.g[at].astype(jnp.float32)
        for more in extra:
            total = total + more.astype(jnp.float32)
        self.g[at] = total.astype(self.g.dtype)

    def send_corner(self):
        def act(zz):
            for copy in self._corner(zz):
                copy.start()

        self.p.planes(act, self.p.depth - 1, 0)
        if self.square:
            self.p.planes(lambda zz: self._square_plane(zz).start(), self.p.depth - 1, 1)

    def send_across(self, far, near):
        def act(zz):
            a, b = self._corner(zz)
            to_x, to_y = self._across(zz)
            a.wait_recv()
            b.wait_recv()
            self._add(self.p.shard(zz, dx=True), self.sides[0], [self.r1[zz, 0]])
            self._add(self.p.shard(zz, dy=True), self.sides[1], [self.r1[zz, 1]])
            to_x.start()
            to_y.start()

        self.p.planes(act, far, near)

    def square_cross(self):
        z, depth = self.p.z, self.p.depth
        at = (pl.ds(z * 4, 4), slice(None), self.square_cols)

        def take(step, total):
            zz = lax.rem(z + step, depth)
            self._square_plane_in(zz).wait_recv()
            return total + self.pz[zz].astype(F32)

        total = lax.fori_loop(1, depth, take, self.g[at].astype(F32))
        for step in range(1, depth):
            self._square_plane(lax.rem(z + step, depth)).wait_send()
        self.g[at] = total.astype(self.g.dtype)
        for copy in self._square_corner():
            copy.start()

    def square_across(self):
        for copy in self._square_corner():
            copy.wait_recv()
        for i in range(2):
            idx = self.p.shard(self.p.z, dx=i == 0, dy=i == 1)
            self._add(idx, self.square_sides[i], [self.p1[i]])
        for copy in self._square_across():
            copy.start()

    def send_planes(self, far, near):
        def act(zz):
            for copy in self._across(zz):
                copy.wait_recv()
            self._add(self.p.shard(zz), self.main_cols, [self.r2[zz, 0], self.r2[zz, 1]])
            self._plane(zz).start()

        self.p.planes(act, far, near)

    def finish(self):
        z, out = self.p.z, self.out
        for copy in self._across(z):
            copy.wait_recv()
        total = self.g[self.p.me, :, self.main_cols].astype(F32)
        out[:, self.main_cols] = total + self.r2[z, 0].astype(F32) + self.r2[z, 1].astype(F32)

        def take(zz):
            self._plane_in(zz).wait_recv()
            out[:, self.main_cols] += self.rz[zz].astype(F32)
            self._plane(zz).wait_send()

        def drain(zz):
            for copy in self._corner(zz) + self._across(zz):
                copy.wait_send()

        self.p.planes(take, self.p.depth - 1, 1)
        self.p.planes(drain, self.p.depth - 1, 0)
        if self.square:
            for copy in self._square_across():
                copy.wait_recv()
            total = self.g[self.p.me, :, self.square_cols].astype(F32)
            out[:, self.square_cols] = total + self.p2[0].astype(F32) + self.p2[1].astype(F32)
            for copy in self._square_corner() + self._square_across():
                copy.wait_send()

    def crossings(self):
        steps = [lambda: self.send_across(self.p.depth - 1, 1), lambda: self.send_across(0, 0)]
        if self.square:
            steps[1] = lambda: (self.send_across(0, 0), self.square_cross())
        return steps

    def lines(self):
        steps = [functools.partial(self.send_planes, far, near) for near, far in reversed(self.p.cuts())]
        if self.square:
            begin = steps[0]
            steps[0] = lambda: (self.square_across(), begin())
        return steps


def scatter_scratch(n, rows, cols, dtype):
    dma = pltpu.SemaphoreType.DMA
    depth = n // 4
    square = cols // 1024 * 128
    main = cols - square
    bufs = [
        pltpu.VMEM((depth, 2, rows, main // 2), dtype),
        pltpu.VMEM((depth, 2, rows, main), dtype),
        pltpu.VMEM((depth, rows, main), dtype),
    ]
    sems = [dma((depth, 2)), dma((depth, 2)), dma((depth, 2)), dma((depth, 2)), dma((depth,)), dma((depth,))]
    if square:
        bufs += [
            pltpu.VMEM((depth, 4, rows, square), dtype),
            pltpu.VMEM((2, rows, square // 2), dtype),
            pltpu.VMEM((2, rows, square), dtype),
        ]
        sems += [dma((depth,)), dma((depth,)), dma((2,)), dma((2,)), dma((2,)), dma((2,))]
    return [pltpu.VMEM((n, rows, cols), dtype), bufs, sems]


VMEM, SMEM, ANY = pltpu.VMEM, pltpu.SMEM, pl.ANY


class Beside:
    def __init__(self):
        self.left = []
        self.done = set()

    def add(self, name, ticks):
        self.left += [(None, tick) for tick in ticks[:-1]] + [(name, ticks[-1])]

    def _next(self):
        name, tick = self.left.pop(0)
        self.done.add(name)
        return tick

    def __call__(self, count=1):
        for _ in range(count):
            if self.left:
                self._next()()

    def in_loop(self, i, steps):
        for step in steps:
            if self.left:
                self._at(i == step, self._next())

    def _at(self, now, tick):
        @pl.when(now)
        def _():
            tick()

    def until(self, name):
        while name not in self.done:
            self()

    def rest(self):
        self(len(self.left))


AHEAD = 3


def gather_stream(beside, jobs, along):
    ticks = [job.ticks() for job in jobs]
    side = along.ticks()

    def both(k):
        ticks[0][k]()
        side[k]()

    steps = [[functools.partial(both, k) for k in range(5)]] + ticks[1:]
    for slot in range(3 * len(jobs) + 2):
        for u, job_steps in enumerate(steps):
            k = slot - 3 * u
            if 0 <= k < 5:
                beside.add(("gathered", u) if k == 4 else None, [job_steps[k]])
            if k == 2 and u + AHEAD < len(jobs):
                beside.add(None, [jobs[u + AHEAD].first])


BAL_END, GIV_END, SHIFT_SEQ, SHIFT_POS, TURN = 0, 4, 8, 12, 16
LOW = jnp.bfloat16
F32 = jnp.float32


def plan_numbers(lengths, seq_order):
    seqs = range(4)
    length = [lengths[j] for j in seqs]
    order = [seq_order[j] for j in seqs]

    def picked(values, place):
        return sum(jnp.where(order[place] == j, values[j], 0) for j in seqs)

    def ends(values):
        return [sum(values[: j + 1]) for j in seqs]

    bal_len = [picked(length, i) for i in seqs]
    bal_end, giv_end = ends(bal_len), ends(length)
    bal_start = [end - size for end, size in zip(bal_end, bal_len)]
    giv_start = [end - size for end, size in zip(giv_end, length)]
    shift_seq = [sum(jnp.where(order[i] == j, bal_start[i], 0) for i in seqs) - giv_start[j] for j in seqs]
    shift_pos = [bal_start[i] - picked(giv_start, i) for i in seqs]
    return bal_end + giv_end + shift_seq + shift_pos + [bal_start[2]]


def places(ends, position, plan):
    seg = jnp.zeros_like(position)
    for j in range(4):
        seg = seg + (position >= plan[ends + j]).astype(jnp.int32)
    return seg


def turned(row, plan, total):
    position = row + plan[TURN]
    return jnp.where(position >= total, position - total, position)


def turned_back(position, plan, total):
    row = position - plan[TURN]
    return jnp.where(row < 0, row + total, row)


def shifted(position, seg, first, plan, sign):
    for j in range(4):
        position = position + sign * jnp.where(seg == j, plan[first + j], 0)
    return position


def column(start, count):
    return start + lax.broadcasted_iota(jnp.int32, (count, 1), 0)


def pick_matrix(index, keep, total):
    lanes = lax.broadcasted_iota(jnp.int32, (index.shape[0], total), 1)
    index = jnp.where(keep, index, -1)
    return jnp.where(lanes == index, 1.0, 0.0).astype(LOW)


def dot(a, b):
    return jnp.dot(a, b, preferred_element_type=F32)


def dot_nt(a, b):
    return lax.dot_general(a, b, (((1,), (1,)), ((), ())), preferred_element_type=F32)


def dot_tn(a, b):
    return lax.dot_general(a, b, (((0,), (0,)), ((), ())), preferred_element_type=F32)


def loop(count, act):
    def step(i, _):
        act(i)
        return 0

    lax.fori_loop(0, count, step, 0)


def part(i, size):
    return pl.ds(pl.multiple_of(i * size, size), size)


def inside(base, i, size):
    return pl.ds(pl.multiple_of(base + i * size, size), size)


def to_partner(src, dst, sems, slot):
    return remote(src, dst, sems.at[0, slot], sems.at[1, slot], {"mp": 1 - lax.axis_index("mp")})


def mean_rows(values):
    return jnp.mean(values, axis=-1, keepdims=True)


CHUNK = 64
TILE = 512
ROW_GAIN, ROW_HIDDEN, ROW_SQUARE, ROW_COUNT, VEC_ROWS = 12, 16, 20, 26, 32


def head_lanes(h, size):
    lanes = lax.broadcasted_iota(jnp.int32, (1, 2 * size), 1)
    mine = lanes < size if h == 0 else lanes >= size
    return jnp.where(mine, 1.0, 0.0).astype(LOW)


def gelu_pair(u):
    rise = 0.5 * (1.0 + lax.erf(u * half_root))
    slope = rise + u * density_scale * jnp.exp(-0.5 * u * u)
    return (u * rise).astype(LOW), slope.astype(LOW)


def norm_chunk(z, gain, shift):
    center = z - mean_rows(z)
    inv = lax.rsqrt(mean_rows(center * center) + layer_eps)
    unit = center * inv
    return unit * gain + shift, unit, inv


def norm_back_chunk(grad, unit, inv, gain):
    scaled = grad * gain
    inner = scaled - mean_rows(scaled) - unit * mean_rows(scaled * unit)
    return inner * inv


def turn_over(src, dst):
    step = 256

    def tile(i):
        dst[:, part(i, step)] = src[part(i, step), :].T

    loop(src.shape[0] // step, tile)


def weight_rows(weight, j, count, cols):
    span = weight.shape[1]
    return weight[part(j, count // span), :, cols].reshape(count, -1)


def weight_cols(weight, cols):
    return weight[:, :, cols].reshape(weight.shape[0] * weight.shape[1], -1)


class Moves:
    def __init__(self, sems):
        self.sems = sems
        self.slots = {}
        self.open = {}

    def start(self, name, src, dst):
        slot = self.slots.setdefault(name, len(self.slots))
        self.open[name] = lambda: pltpu.make_async_copy(src, dst, self.sems.at[slot])
        self.open[name]().start()

    def wait(self, *names):
        for name in names:
            if name in self.open:
                self.open.pop(name)().wait()

    def wait_all(self):
        self.wait(*list(self.open))


def forward_kernel(n, stride, sizes, *refs):
    rows, total, width, cols, hidden = sizes
    units = 3 * LAYERS
    refs = list(refs)

    def take(count):
        taken = refs[:count]
        del refs[:count]
        return taken

    lengths, seq_order, x, cot, w_qkv, w_out, w_in, w_back, biases, gains, hidden_bias = take(11)
    x_out, qm_out, probs_out, y_out, act_out, slope_out, unit_out, inv_out = take(8)
    weights = take(units)
    vec, squares, dh = take(3)
    first_src, small, small_all = take(3)
    xs, qm, probs, wa, wi, wb, y_all, act, slope, unit, inv, stream, yf, held, sent, got, bias = take(17)
    pair_sems, move_sems, probs_sems, gather_sems = take(4)
    core = lax.axis_index("mp")
    base, other = core * rows, (1 - core) * rows
    own = part(core, rows)
    half = total // 2
    size = HEAD_DIM
    pair = 2 * size
    scale = HEAD_DIM ** (-0.5)
    slabs = cols // pair
    place = Place(n, stride)
    *gather_sems, own_sems = gather_sems
    plan = plan_numbers(lengths, seq_order)

    def pack_first(layer):
        for i in range(3):
            first_src[layer, :, pl.ds(i * cols, cols)] = w_qkv[layer, i]
        first_src[layer, :, pl.ds(3 * cols, cols)] = w_out[layer]

    pack_first(0)
    small[...] = jnp.zeros_like(small)
    span = w_in.shape[1]
    for layer in range(LAYERS):
        for row, values in ((6 * layer, biases), (ROW_GAIN + 2 * layer, gains), (ROW_HIDDEN + 2 * layer, hidden_bias)):
            for i in range(6 if values is biases else values.shape[1]):
                value = values[i, layer : layer + 1] if values is biases else values[layer, i : i + 1]
                small[row + i : row + i + 1, pl.ds(0, span)] = value.astype(F32)
    shards = []
    for layer in range(LAYERS):
        shards += [first_src.at[layer], w_in.at[layer], w_back.at[layer]]
    jobs = []
    for u, (src, dst) in enumerate(zip(shards + [small], weights + [small_all])):
        sems = [sem.at[u] for sem in gather_sems]
        jobs.append(Gather(place, src, dst, u % 2, sems[:2], sems[2:], own_sems.at[u]))
    greet(place, False)
    little = jobs.pop()
    little.first()
    for job in jobs[:AHEAD]:
        job.first()
    beside = Beside()
    gather_stream(beside, jobs, little)
    moves = Moves(move_sems)
    for layer in range(1, LAYERS):
        pack_first(layer)

    def fetch(u, where):
        beside.until(("gathered", u))
        moves.start(where, weights[u], {"wa": wa, "wi": wi, "wb": wb}[where])

    x_given, cot_given = pl.ds(0, width), pl.ds(width, width)
    copies = [
        to_partner(x, act.at[own, x_given], pair_sems, 4),
        to_partner(cot, act.at[own, cot_given], pair_sems, 5),
    ]
    for copy in copies:
        copy.start()
    act[own, x_given] = x[...]
    act[own, cot_given] = cot[...]
    squares[...] = jnp.zeros_like(squares)
    for copy in copies:
        copy.wait()
    beside()

    def turn(i):
        index = turned(column(i * TILE, TILE), plan, total)
        picks = pick_matrix(index, index >= 0, total)
        xs[0, part(i, TILE), :] = dot(picks, act[:, x_given]).astype(LOW)

    loop(total // TILE, turn)
    moves.start("x", xs.at[0], x_out.at[0])
    beside()
    position = turned(column(base, rows), plan, total)
    seg = places(BAL_END, position, plan)
    target = shifted(position, seg, SHIFT_POS, plan, -1)
    dh[...] = dot(pick_matrix(target, seg < 4, total), act[:, cot_given]).astype(LOW)
    stream[...] = xs[0, own, :].astype(F32)
    fetch(0, "wa")

    per = 128 // span
    from_lane = lax.broadcasted_iota(jnp.int32, (128, 128), 0)
    to_lane = lax.broadcasted_iota(jnp.int32, (128, 128), 1)

    def spread(j):
        lanes = 0.0
        for i in range(per):
            shift = jnp.where(to_lane == from_lane + i * span, 1.0, 0.0).astype(LOW)
            lanes = lanes + dot(small_all[j * per + i, :, pl.ds(0, 128)].astype(LOW), shift)
        vec[:, part(j, 128)] = lanes

    loop(width // 128, spread)

    back = turned(column(half, half), plan, total)
    seg_k = places(BAL_END, back, plan)
    across = turned(half + lax.broadcasted_iota(jnp.int32, (1, half), 1), plan, total)
    seg_q = places(BAL_END, across, plan)

    def valid(i):
        return places(BAL_END, turned(column(base + i * CHUNK, CHUNK), plan, total), plan) < 4

    for layer in range(LAYERS):
        x_all = xs.at[layer % 2]
        next_all = xs.at[(layer + 1) % 2]
        row = 6 * layer
        gain = ROW_GAIN + 2 * layer
        head_span = part(core, cols)
        bias[...] = jnp.zeros_like(bias)
        bias[0:1, pl.ds(0, cols)] = vec[row : row + 1, head_span]
        bias[0:1, pl.ds(2 * cols, cols)] = vec[row + 1 : row + 2, head_span]
        moves.wait_all()

        def project(t):
            m, j = lax.div(t, 3), lax.rem(t, 3)
            acc = dot(x_all[part(m, TILE), :], weight_cols(wa, part(j, cols)))
            qm[part(m, TILE), part(j, cols)] = (acc + bias[0:1, part(j, cols)]).astype(LOW)
            beside.in_loop(t, [3])

        loop(3 * (total // TILE), project)
        beside()

        def probs_move(s):
            slot = s % 2 if isinstance(s, int) else lax.rem(s, 2)
            return pltpu.make_async_copy(probs.at[slot], probs_out.at[layer, s], probs_sems.at[slot])

        def slab(s):
            slot = lax.rem(s, 2)

            @pl.when(s >= 2)
            def _():
                probs_move(s - 2).wait()

            for b in range(2):
                at = pl.ds(b * half, half)
                q = qm[at, part(s, pair)]
                k = qm[at, inside(cols, s, pair)]
                v = qm[at, inside(2 * cols, s, pair)]
                mixed = []
                for h in range(2):
                    lanes = head_lanes(h, size)
                    scores = dot_nt(k, q * (lanes * scale))
                    if b == 1:
                        scores = jnp.where(seg_k == seg_q, scores, -1e30)
                    peak = jnp.max(scores, axis=0, keepdims=True)
                    powers = jnp.exp(scores - peak)
                    share = (powers * (1.0 / jnp.sum(powers, axis=0, keepdims=True))).astype(LOW)
                    probs[slot, b, pl.ds(h * half, half), :] = share
                    mixed.append(dot_tn(v, share)[h * size : (h + 1) * size, :])
                qm[at, inside(3 * cols, s, pair)] = jnp.concatenate(mixed, axis=0).T.astype(LOW)
            probs_move(s).start()
            beside.in_loop(s, range(slabs))

        loop(slabs, slab)
        moves.start("qm", qm, qm_out.at[layer])
        for s in range(max(slabs - 2, 0), slabs):
            probs_move(s).wait()

        def out_of(left, left_cols, right, right_cols, slot):
            def product(at, j):
                return dot_nt(left[at, left_cols], weight_rows(right, j, TILE, right_cols))

            def far(j):
                sent[slot, :, part(j, TILE)] = product(part(1 - core, rows), j).astype(LOW)

            loop(width // TILE, far)
            copy = to_partner(sent.at[slot], got.at[slot], pair_sems, slot)
            copy.start()
            beside()

            def near(j):
                held[:, part(j, TILE)] = product(own, j)

            loop(width // TILE, near)
            copy.wait()

        mix_cols = pl.ds(3 * cols, cols)
        out_of(qm, mix_cols, wa, mix_cols, 0)

        def first_norm(i):
            at = part(i, CHUNK)
            h = stream[at, :]
            a = held[at, :] + got[0, at, :].astype(F32) + vec[row + 2 : row + 3, :]
            ok = jnp.where(valid(i), 1.0, 0.0)
            squares[3 * layer : 3 * layer + 1, :] += jnp.sum(ok * h * h, axis=0, keepdims=True)
            squares[3 * layer + 1 : 3 * layer + 2, :] += jnp.sum(ok * a * a, axis=0, keepdims=True)
            y, z, r = norm_chunk(h + a, vec[gain : gain + 1, :], vec[row + 3 : row + 4, :])
            unit[0, at, :] = z
            inv[0, at, :] = jnp.broadcast_to(r, (CHUNK, 128))
            yf[at, :] = y
            y_all[inside(base, i, CHUNK), :] = y.astype(LOW)

        loop(rows // CHUNK, first_norm)
        y_copy = to_partner(y_all.at[own], y_all.at[own], pair_sems, 2)
        y_copy.start()
        fetch(3 * layer + 1, "wi")
        moves.wait("wi")

        def raise_rows(start, at_steps):
            def tile(t):
                at, col = pl.ds(pl.multiple_of(start, rows), rows), part(t, TILE)
                hidden_row = ROW_HIDDEN + 2 * layer + lax.div(t, width // TILE)
                shift = vec[pl.ds(hidden_row, 1), part(lax.rem(t, width // TILE), TILE)]
                value, grad = gelu_pair(dot(y_all[at, :], weight_cols(wi, col)) + shift)
                act[at, col] = value
                slope[at, col] = grad
                beside.in_loop(t, at_steps)

            loop(hidden // TILE, tile)

        raise_rows(base, [1, 3])
        y_copy.wait()
        moves.start("y", y_all, y_out.at[layer])
        raise_rows(other, [1, 3] if layer + 1 < LAYERS else [3])
        moves.start("act", act, act_out.at[layer])
        moves.start("slope", slope, slope_out.at[layer])
        fetch(3 * layer + 2, "wb")
        moves.wait("wb")
        out_of(act, slice(None), wb, slice(None), 1)
        beside()

        def second_norm(i):
            at = part(i, CHUNK)
            f = held[at, :] + got[1, at, :].astype(F32) + vec[row + 4 : row + 5, :]
            ok = jnp.where(valid(i), 1.0, 0.0)
            squares[3 * layer + 2 : 3 * layer + 3, :] += jnp.sum(ok * f * f, axis=0, keepdims=True)
            h, z, r = norm_chunk(yf[at, :] + f, vec[gain + 1 : gain + 2, :], vec[row + 5 : row + 6, :])
            unit[1, at, :] = z
            inv[1, at, :] = jnp.broadcast_to(r, (CHUNK, 128))
            stream[at, :] = h
            next_all[inside(base, i, CHUNK), :] = h.astype(LOW)

        loop(rows // CHUNK, second_norm)
        moves.start("unit", unit, unit_out.at[layer])
        moves.start("inv", inv, inv_out.at[layer])
        if layer + 1 < LAYERS:
            pass_on = to_partner(next_all.at[own], next_all.at[own], pair_sems, 3)
            pass_on.start()
            fetch(3 * layer + 3, "wa")
            pass_on.wait()
            moves.start("x", next_all, x_out.at[layer + 1])
        else:
            pass_on = to_partner(next_all.at[own], x_out.at[LAYERS, own], pair_sems, 3)
            pass_on.start()
            moves.start("x", next_all.at[own], x_out.at[LAYERS, own])
            pass_on.wait()
    beside.rest()
    for job in [little] + jobs:
        job.drain()
    moves.wait_all()


def forward(lengths, seq_order, x, cot, weights, vectors, n, stride, part_count):
    rows, width = x.shape
    total = rows * part_count
    span, hidden = weights[2].shape[1:]
    cols = weights[0].shape[3]
    shape = jax.ShapeDtypeStruct
    units = 3 * LAYERS
    half = total // 2
    slabs = cols // (2 * HEAD_DIM)
    dma = pltpu.SemaphoreType.DMA
    depth = n // 4
    vmem, smem, far = [pl.BlockSpec(memory_space=where) for where in (VMEM, SMEM, ANY)]
    outs = [
        shape((LAYERS + 1, total, width), LOW),
        shape((LAYERS, total, 4 * cols), LOW),
        shape((LAYERS, slabs, 2, 2 * half, half), LOW),
        shape((LAYERS, total, width), LOW),
        shape((LAYERS, total, hidden), LOW),
        shape((LAYERS, total, hidden), LOW),
        shape((LAYERS, 2, rows, width), F32),
        shape((LAYERS, 2, rows, 128), F32),
    ]
    outs += [shape((n, span, hidden), LOW)] * units
    outs += [
        shape((VEC_ROWS, width), F32),
        shape((8, width), F32),
        shape((rows, width), LOW),
    ]
    results = pl.pallas_call(
        functools.partial(forward_kernel, n, stride, (rows, total, width, cols, hidden)),
        out_shape=outs,
        in_specs=[smem, smem, vmem, vmem, vmem, vmem, far, far, vmem, vmem, vmem],
        out_specs=[far] * (8 + units) + [vmem] * 3,
        scratch_shapes=[
            VMEM((LAYERS, span, hidden), LOW),
            VMEM((VEC_ROWS, 256), F32),
            VMEM((n, VEC_ROWS, 256), F32),
            VMEM((2, total, width), LOW),
            VMEM((total, 4 * cols), LOW),
            VMEM((2, 2, 2 * half, half), LOW),
            VMEM((n, span, hidden), LOW),
            VMEM((n, span, hidden), LOW),
            VMEM((n, span, hidden), LOW),
            VMEM((total, width), LOW),
            VMEM((total, hidden), LOW),
            VMEM((total, hidden), LOW),
            VMEM((2, rows, width), F32),
            VMEM((2, rows, 128), F32),
            VMEM((rows, width), F32),
            VMEM((rows, width), F32),
            VMEM((rows, width), F32),
            VMEM((2, rows, width), LOW),
            VMEM((2, rows, width), LOW),
            VMEM((8, 3 * cols), F32),
            dma((2, 6)),
            dma((12,)),
            dma((2,)),
            [
                dma((units + 1, ColumnFirst.SENDS, depth)),
                dma((units + 1, ColumnFirst.RECVS, depth)),
                dma((units + 1, 4)),
                dma((units + 1, 4)),
                dma((units + 1, 2, 4, depth)),
                dma((units + 1, 4, depth)),
                dma((units + 1,)),
            ],
        ],
        compiler_params=pltpu.CompilerParams(
            collective_id=0, has_side_effects=True, vmem_limit_bytes=62 << 20
        ),
        name="forward",
    )(lengths, seq_order, x, cot, *weights, *vectors)
    return results[:8], results[8 : 8 + units], results[8 + units :]


def backward_kernel(n, stride, slot_count, sizes, *refs):
    rows, total, width, cols, hidden = sizes
    units = 3 * LAYERS
    refs = list(refs)

    def take(count):
        taken = refs[:count]
        del refs[:count]
        return taken

    lengths, seq_order, vec, squares, dh_in = take(5)
    plan = plan_numbers(lengths, seq_order)
    x_far, qm_far, probs_far, y_far, act_far, slope_far, unit_far, inv_far = take(8)
    weights = take(units)
    output, input_grad, grad_qkv, grad_out, grad_in, grad_back = take(6)
    own_small, partner_small = take(2)
    w1, w2, h1, h2, n1, sides, flip, probs = take(8)
    unit_rows, inv, dz, dh, sent, got, grads, staged = take(8)
    pair_sems, move_sems, probs_sems, read_sem = take(4)
    slots = take(slot_count)
    (little_refs,) = take(1)
    core = lax.axis_index("mp")
    base, other = core * rows, (1 - core) * rows
    own = part(core, rows)
    half = total // 2
    size = HEAD_DIM
    pair = 2 * size
    scale = HEAD_DIM ** (-0.5)
    slabs = cols // pair
    span = width // n
    place = Place(n, stride)
    moves = Moves(move_sems)
    crossings, lines = Beside(), Beside()
    jobs = [Scatter(place, staged, *slots[u % slot_count]) for u in range(units)]
    little = Scatter(place, own_small, *little_refs)

    def load_norm(layer):
        moves.start("unit", unit_far.at[layer, 1], unit_rows)
        moves.start("inv", inv_far.at[layer], inv)

    def free(u):
        if u >= slot_count:
            end(u - slot_count)

    def cross(u):
        crossings.until(u)

    def line(u, stage):
        crossings.until(u)
        lines.until((u, stage))

    def end(u):
        crossings.until(u)
        lines.until(u)

    def summed(u):
        job = jobs[u]
        job.send_corner()

        layer = last - u // 3
        if u % 3 == 2:
            targets = [(job.out.at[:, pl.ds(i * cols, cols)], grad_qkv.at[layer, i]) for i in range(3)]
            targets.append((job.out.at[:, pl.ds(3 * cols, cols)], grad_out.at[layer]))
        else:
            targets = [(job.out, (grad_back, grad_in)[u % 3].at[layer])]
        names = ["staged%d" % i for i in range(4)]

        def leave():
            moves.wait(*names)
            job.finish()
            for name, target in zip(names, targets):
                moves.start(name, *target)

        crossings.add(u, job.crossings())
        for stage, tick in enumerate(job.lines()):
            lines.add((u, stage), [tick])
        lines.add(u, [leave])

    last = LAYERS - 1
    moves.start("dh", dh_in, sent)
    load_norm(last)
    moves.start("w2", weights[3 * last + 2], w2)
    moves.start("h2", slope_far.at[last], h2)
    moves.start("h1", act_far.at[last], h1)
    moves.start("w1", weights[3 * last + 1], w1)
    moves.start("n1", y_far.at[last], n1)
    greet(place, True)
    grads[...] = jnp.zeros_like(grads)
    moves.wait("dh")

    def widen(i):
        dh[part(i, CHUNK), :] = sent[part(i, CHUNK), :].astype(F32)

    loop(rows // CHUNK, widen)

    def add_sum(row, values, lanes=slice(None)):
        grads[row : row + 1, lanes] += jnp.sum(values, axis=0, keepdims=True)

    for layer in reversed(range(LAYERS)):
        row = 6 * layer
        gain = ROW_GAIN + 2 * layer
        unit = 3 * (last - layer)
        moves.wait("unit", "inv")

        def second_norm(i):
            at = part(i, CHUNK)
            grad, z = dh[at, :], unit_rows[at, :]
            add_sum(gain + 1, grad * z)
            add_sum(row + 5, grad)
            out = norm_back_chunk(grad, z, inv[1, at, 0:1], vec[gain + 1 : gain + 2, :])
            dz[at, :] = out
            df = out.astype(LOW)
            add_sum(row + 4, df.astype(F32))
            sides[inside(base, i, CHUNK), :] = df

        loop(rows // CHUNK, second_norm)
        moves.start("unit", unit_far.at[layer, 0], unit_rows)
        if unit:
            pl.semaphore_wait(read_sem, 1)
        df_copy = to_partner(sides.at[own], sides.at[own], pair_sems, 0)
        df_copy.start()
        moves.wait("w2", "h2")

        def hidden_rows(start):
            def tile(t):
                at, col = pl.ds(pl.multiple_of(start, rows), rows), part(t, TILE)
                grad = (dot(sides[at, :], weight_cols(w2, col)) * h2[at, col].astype(F32)).astype(LOW)
                h2[at, col] = grad
                hidden_row = ROW_HIDDEN + 2 * layer + lax.div(t, width // TILE)
                grads[pl.ds(hidden_row, 1), part(lax.rem(t, width // TILE), TILE)] += jnp.sum(
                    grad.astype(F32), axis=0, keepdims=True
                )

            loop(hidden // TILE, tile)

        hidden_rows(base)
        df_copy.wait()
        turn_over(sides, flip)
        shards = TILE // span

        def outer(g, right, right_cols, g_cols, count, step):
            def tile(t):
                m, j = lax.div(t, count), lax.rem(t, count)
                value = dot(flip[part(m, TILE), :], right[:, inside(right_cols, j, step)])
                g[part(m, shards), :, inside(g_cols, j, step)] = value.astype(LOW).reshape(shards, span, step)

            loop((width // TILE) * count, tile)

        moves.wait("h1")
        free(unit)
        outer(jobs[unit].g, h1, 0, 0, hidden // TILE, TILE)
        summed(unit)
        if unit:
            line(unit - 2, 0)
        moves.start("h1", qm_far.at[layer], h1)
        hidden_rows(other)
        moves.start("w2", weights[3 * layer], w2)
        moves.wait("w1")

        def product(at, left, left_cols, right, right_cols, j):
            return dot_nt(left[at, left_cols], weight_rows(right, j, TILE, right_cols))

        every = slice(None)

        def far(j):
            sent[:, part(j, TILE)] = product(part(1 - core, rows), h2, every, w1, every, j).astype(LOW)

        loop(width // TILE, far)
        dy_copy = to_partner(sent, got, pair_sems, 1)
        dy_copy.start()

        def near(j):
            dh[:, part(j, TILE)] = product(own, h2, every, w1, every, j)

        loop(width // TILE, near)
        if unit:
            line(unit - 2, 1)
        moves.wait("unit")
        dy_copy.wait()

        def first_norm(i):
            at = part(i, CHUNK)
            grad, z = dz[at, :] + dh[at, :] + got[at, :].astype(F32), unit_rows[at, :]
            add_sum(gain, grad * z)
            add_sum(row + 3, grad)
            out = norm_back_chunk(grad, z, inv[0, at, 0:1], vec[gain : gain + 1, :])
            dz[at, :] = out
            da = out.astype(LOW)
            add_sum(row + 2, da.astype(F32))
            sides[inside(base, i, CHUNK), :] = da

        loop(rows // CHUNK, first_norm)
        da_copy = to_partner(sides.at[own], sides.at[own], pair_sems, 2)
        da_copy.start()
        if layer:
            load_norm(layer - 1)
            moves.start("w1", weights[3 * layer - 2], w1)
        if unit:
            line(unit - 2, 2)
            cross(unit - 1)
        else:
            cross(unit)
        free(unit + 1)
        moves.wait("n1")
        turn_over(n1, flip)
        moves.start("n1", x_far.at[layer], n1)
        outer(jobs[unit + 1].g, h2, 0, 0, hidden // TILE, TILE)
        summed(unit + 1)
        da_copy.wait()
        moves.wait("w2", "h1")
        mix_cols = pl.ds(3 * cols, cols)

        def probs_move(s, b):
            return pltpu.make_async_copy(probs_far.at[layer, s, b], probs.at[b], probs_sems.at[b])

        for b in range(2):
            probs_move(0, b).start()

        def mix_grad(m):
            value = dot(sides[part(m, TILE), :], weight_cols(w2, mix_cols))
            h2[part(m, TILE), mix_cols] = value.astype(LOW)

        loop(total // TILE, mix_grad)

        def slab(s):
            for b in range(2):
                at = pl.ds(b * half, half)
                q = h1[at, part(s, pair)]
                k = h1[at, inside(cols, s, pair)]
                v = h1[at, inside(2 * cols, s, pair)]
                do = h2[at, inside(3 * cols, s, pair)]
                inner = (do.astype(F32) * h1[at, inside(3 * cols, s, pair)].astype(F32)).T
                probs_move(s, b).wait()
                dq, dk, dv = [], 0.0, 0.0
                for h in range(2):
                    lanes = head_lanes(h, size)
                    mine = do * lanes
                    share = probs[b, pl.ds(h * half, half), :]
                    rowsum = jnp.sum(inner[h * size : (h + 1) * size, :], axis=0, keepdims=True)
                    ds = (share.astype(F32) * (dot_nt(v, mine) - rowsum)).astype(LOW)
                    dk = dk + dot(ds, q * (lanes * scale))
                    dv = dv + dot(share, mine)
                    dq.append(dot_tn(k, ds)[h * size : (h + 1) * size, :])

                @pl.when(s + 1 < slabs)
                def _(b=b):
                    probs_move(s + 1, b).start()

                dq = (jnp.concatenate(dq, axis=0) * scale).T.astype(LOW)
                dk, dv = dk.astype(LOW), dv.astype(LOW)
                h2[at, part(s, pair)] = dq
                h2[at, inside(cols, s, pair)] = dk
                h2[at, inside(2 * cols, s, pair)] = dv
                lanes_here = inside(core * cols, s, pair)
                add_sum(row, dq.astype(F32), lanes_here)
                add_sum(row + 1, dv.astype(F32), lanes_here)
            if unit:
                crossings.in_loop(s, [0, 0])
            lines.in_loop(s, [1, 2, 3])

        loop(slabs, slab)
        qkv_cols = pl.ds(0, 3 * cols)

        def far_input(j):
            value = product(part(1 - core, rows), h2, qkv_cols, w2, qkv_cols, j)
            sent[:, part(j, TILE)] = value.astype(LOW)

        loop(width // TILE, far_input)
        dh_copy = to_partner(sent, got, pair_sems, 3)
        dh_copy.start()

        def near_input(j):
            at = part(j, TILE)
            dh[:, at] = dz[:, at] + product(own, h2, qkv_cols, w2, qkv_cols, j)

        loop(width // TILE, near_input)
        if layer:
            moves.start("w2", weights[3 * layer - 1], w2)
        cross(unit + 1)
        free(unit + 2)
        g = jobs[unit + 2].g
        turn_over(sides, flip)
        if layer:
            pl.semaphore_signal(
                read_sem, inc=1, device_id={"mp": 1 - core}, device_id_type=MESH
            )
        outer(g, h1, 3 * cols, 3 * cols, 1, cols)
        if layer:
            moves.start("h1", act_far.at[layer - 1], h1)
        moves.wait("n1")
        turn_over(n1, flip)
        moves.start("n1", y_far.at[layer - 1] if layer else x_far.at[LAYERS], n1)
        outer(g, h2, 0, 0, 3, cols)
        summed(unit + 2)
        if layer:
            moves.start("h2", slope_far.at[layer - 1], h2)
        dh_copy.wait()

        def add_got(i):
            dh[part(i, CHUNK), :] += got[part(i, CHUNK), :].astype(F32)

        loop(rows // CHUNK, add_got)

    totals = jnp.sum(squares[0 : 3 * LAYERS, :], axis=1, keepdims=True)
    grads[ROW_SQUARE : ROW_SQUARE + 3 * LAYERS, :] = jnp.broadcast_to(totals, (3 * LAYERS, width))
    count = jnp.full((1, width), plan[BAL_END + 3], jnp.int32).astype(F32)
    grads[ROW_COUNT : ROW_COUNT + 1, :] = count
    per = 128 // span
    little.g[...] = jnp.zeros_like(little.g)

    def cut(j):
        lanes = grads[:, part(j, 128)]
        for i in range(per):
            little.g[j * per + i, :, pl.ds(0, 128)] = lanes

    loop(width // 128, cut)
    little.send_corner()

    dh_copy = to_partner(dh, unit_rows, pair_sems, 0)
    dh_copy.start()
    line(units - 3, 2)
    step = rows // 4
    moves.wait("n1")

    def give(i):
        given = column(base + i * step, step)
        seg = places(GIV_END, given, plan)
        source = turned_back(shifted(given, seg, SHIFT_SEQ, plan, 1), plan, total)
        sent[part(i, step), :] = dot(pick_matrix(source, seg < 4, total), n1[...]).astype(LOW)

    loop(4, give)
    moves.start("output", sent, output)
    dh_copy.wait()
    low_cols = pl.ds(0, width)

    def split(i):
        for start, values in ((base, dh), (other, unit_rows)):
            value = values[part(i, CHUNK), :]
            top = value.astype(LOW)
            at = inside(start, i, CHUNK)
            sides[at, :] = top
            h1[at, low_cols] = (value - top.astype(F32)).astype(LOW)

    loop(rows // CHUNK, split)

    def turn_back(i):
        back = turned_back(column(base + i * step, step), plan, total)
        picks = pick_matrix(back, back >= 0, total)
        dz[part(i, step), :] = dot(picks, sides[...]) + dot(picks, h1[:, low_cols])

    loop(4, turn_back)
    moves.start("input_grad", dz, input_grad)
    little_ticks = little.crossings() + little.lines() + [little.finish]
    for tick in little_ticks[:2]:
        tick()
    end(units - 3)
    cross(units - 1)
    for tick in little_ticks[2:]:
        tick()
    swap = to_partner(own_small, partner_small, pair_sems, 1)
    swap.start()
    end(units - 1)
    swap.wait()
    moves.wait_all()


def backward(lengths, seq_order, vec, squares, dh, kept, weights, n, stride):
    rows, width = dh.shape
    total, hidden = kept[4].shape[1:]
    slot_count = 3 if n <= 16 else 2
    span = weights[0].shape[1]
    cols = kept[1].shape[2] // 4
    units = len(weights)
    half = total // 2
    shape = jax.ShapeDtypeStruct
    dma = pltpu.SemaphoreType.DMA
    vmem, smem, far = [pl.BlockSpec(memory_space=where) for where in (VMEM, SMEM, ANY)]
    outs = [shape((rows, width), LOW), shape((rows, width), F32)]
    outs += [
        shape((LAYERS, 3, span, cols), F32),
        shape((LAYERS, span, cols), F32),
        shape((LAYERS, span, hidden), F32),
        shape((LAYERS, span, hidden), F32),
    ]
    outs += [shape((VEC_ROWS, 256), F32)] * 2
    results = pl.pallas_call(
        functools.partial(backward_kernel, n, stride, slot_count, (rows, total, width, cols, hidden)),
        out_shape=outs,
        in_specs=[smem, smem, vmem, vmem] + [far] * (9 + units),
        out_specs=[far] * 6 + [vmem] * 2,
        scratch_shapes=[
            VMEM((n, span, hidden), LOW),
            VMEM((n, span, hidden), LOW),
            VMEM((total, hidden), LOW),
            VMEM((total, hidden), LOW),
            VMEM((total, width), LOW),
            VMEM((total, width), LOW),
            VMEM((width, total), LOW),
            VMEM((2, 2 * half, half), LOW),
            VMEM((rows, width), F32),
            VMEM((2, rows, 128), F32),
            VMEM((rows, width), F32),
            VMEM((rows, width), F32),
            VMEM((rows, width), LOW),
            VMEM((rows, width), LOW),
            VMEM((VEC_ROWS, width), F32),
            VMEM((span, hidden), F32),
            dma((2, 4)),
            dma((20,)),
            dma((2,)),
            pltpu.SemaphoreType.REGULAR,
        ]
        + [scatter_scratch(n, span, hidden, LOW)] * slot_count
        + [scatter_scratch(n, VEC_ROWS, 256, F32)],
        compiler_params=pltpu.CompilerParams(
            collective_id=1, has_side_effects=True, vmem_limit_bytes=63 << 20
        ),
        name="backward",
    )(lengths, seq_order, vec, squares, dh, *kept, *weights)
    return results[:2], results[2:6], results[6:]


def grouped(values, stride, own):
    total = values
    for step in range(1, stride):
        n = lax.axis_size("dp")
        pairs = [(i, i - i % stride + (i + step) % stride) for i in range(n)]
        total = total + lax.ppermute(values, "dp", pairs)
    return total


def body(
    inputs,
    cotangent,
    lengths,
    seq_order,
    w_qkv,
    w_out,
    w_in,
    w_back,
    biases,
    norm_gains,
    hidden_bias,
):
    devices = lax.axis_size("dp")
    part_count = lax.axis_size("mp")
    width = inputs.shape[1]
    span = biases.shape[2]
    cols = w_qkv.shape[3]
    stride = max(1, 16 // span)
    n = devices // stride
    place_here = lax.axis_index("dp")

    def shared(values, axis):
        if stride == 1:
            return values
        shape = list(values.shape)
        size = shape[axis]
        shape[axis] = size * stride
        start = lax.rem(place_here, stride) * size
        return grouped(lax.dynamic_update_slice_in_dim(jnp.zeros(shape, values.dtype), values, start, axis), stride, 0)

    turned_out, turned_back = jnp.swapaxes(w_out, 1, 2), jnp.swapaxes(w_back, 1, 2)
    weights = [shared(w_qkv, 2), shared(turned_out, 1), shared(w_in, 1), shared(turned_back, 1)]
    vectors = [shared(vector, 2) for vector in (jnp.swapaxes(biases, 0, 1), norm_gains, hidden_bias)]
    lengths, seq_order = lengths.reshape(-1), seq_order.reshape(-1)
    kept, gathered, (vec, squares, dh) = forward(
        lengths, seq_order, inputs, cotangent, weights, vectors, n, stride, part_count
    )
    (output, input_grad), sums, (own_small, partner_small) = backward(
        lengths, seq_order, vec, squares, dh, kept, gathered, n, stride
    )

    if stride > 1:
        start = lax.rem(place_here, stride) * span
        sums = [lax.dynamic_slice_in_dim(grouped(sum_, stride, 0), start, span, sum_.ndim - 2) for sum_ in sums]
        own_small, partner_small = grouped(own_small, stride, 0), grouped(partner_small, stride, 0)
    both = own_small + partner_small
    lane = lax.rem(place_here, 128 // span) * span

    def lanes(values):
        return lax.dynamic_slice_in_dim(values, lane, span, 1)

    grad_biases = lanes(both[:ROW_GAIN]).reshape(biases.shape)
    grad_gains = lanes(both[ROW_GAIN:ROW_HIDDEN]).reshape(norm_gains.shape)
    grad_hidden_bias = lanes(own_small[ROW_HIDDEN:ROW_SQUARE]).reshape(hidden_bias.shape)
    valid_count = both[ROW_COUNT, 0] / part_count
    rms = jnp.sqrt(both[ROW_SQUARE:ROW_COUNT, 0] / (valid_count * width)).reshape(LAYERS, 3)

    grad_qkv, grad_out, grad_in, grad_back = sums
    grad_out, grad_back = jnp.swapaxes(grad_out, 1, 2), jnp.swapaxes(grad_back, 1, 2)
    return (
        output,
        input_grad,
        grad_qkv,
        grad_out,
        grad_in,
        grad_back,
        grad_biases,
        grad_gains,
        grad_hidden_bias,
        rms,
    )


def solution(mesh):
    in_specs = (
        P(("dp", "mp"), None),
        P(("dp", "mp"), None),
        P("dp", None),
        P("dp", None),
        P(None, None, "dp", "mp"),
        P(None, "mp", "dp"),
        P(None, "dp", "mp"),
        P(None, "mp", "dp"),
        P(None, None, "dp"),
        P(None, None, "dp"),
        P(None, "mp", "dp"),
    )
    out_specs = (
        P(("dp", "mp"), None),
        P(("dp", "mp"), None),
        P(None, None, "dp", "mp"),
        P(None, "mp", "dp"),
        P(None, "dp", "mp"),
        P(None, "mp", "dp"),
        P(None, None, "dp"),
        P(None, None, "dp"),
        P(None, "mp", "dp"),
        P(),
    )
    return jax.shard_map(body, mesh=mesh, in_specs=in_specs, out_specs=out_specs, check_vma=False)
```
